32 devices in a mesh: tm: 8 (over z, x), height: 2 (over y), dp: 2 (over core).
Axes of the slice: x: 2, y: 2, z: 4, core: 2. Of those that a mesh axis runs over, the one named last changes fastest.
Arguments:
- frames_in: bfloat16 [2, 32, 8, 48, 256], P('dp', 'tm', 'height'), may hold values from -6 to 6
- cotangent: bfloat16 [2, 32, 8, 48, 256], P('dp', 'tm', 'height'), may hold values from -6 to 6
- w_spatial: bfloat16 [3, 3, 256, 256], replicated, may hold values from -0.125 to 0.125
- w_temporal: bfloat16 [3, 256, 256], replicated, may hold values from -0.21875 to 0.21875
Outputs:
- decoded: bfloat16 [2, 32, 8, 48, 256], P('dp', 'tm', 'height')
- input_grad: bfloat16 [2, 32, 8, 48, 256], P('dp', 'tm', 'height')
- spatial_grad: bfloat16 [3, 3, 256, 256], replicated
- temporal_grad: bfloat16 [3, 256, 256], replicated
The draws below stay inside these ranges and needn't reach their ends.
All inputs are finite; a program needn't handle non-finite values.
Results may differ from the reference program's by a relative error of at most 0.0061.
Values may be sent and summed in bfloat16 or wider, within the bound.
A program may use at most 64 MiB of HBM per device.

```python
import math
import jax
import jax.numpy as jnp
from jax import lax

CH = 256
COLS = 48
FRAMES = 32
ROWS = 8
CELLS = 24576
N_DP = 2


def levels(key, shape, cuts, least, top_value):
    def one(axis_at, shards_of):
        heights = jax.random.uniform(jax.random.fold_in(jax.random.fold_in(key, 6), axis_at), (shards_of,), jnp.float32, least / len(cuts), top_value / len(cuts))
        return jnp.repeat(jnp.exp(heights), shape[axis_at] // shards_of).reshape((-1,) + (1,) * (len(shape) - axis_at - 1))

    level = one(*cuts[0])
    for cut in cuts[1:]:
        level = level * one(*cut)
    return level


def bell_draw(rng, dims, scale, most, cuts=(), kind=jnp.bfloat16):
    drawn = jax.random.normal(rng, dims, jnp.float32) * scale
    if len(cuts) > 0:
        drawn = levels(rng, dims, cuts, -0.22, 0.18) * drawn
    return jnp.clip(drawn, min=-most, max=most).astype(kind)


def setup_inputs(seed: int = 0) -> dict:
    arg_keys = jax.random.split(jax.random.key(seed), 5)
    return {
        "frames_in": bell_draw(arg_keys[0], (N_DP, FRAMES, ROWS, COLS, CH), 1.0, 6.0, ((0, 2), (1, 8), (2, 2))),
        "cotangent": bell_draw(arg_keys[1], (N_DP, FRAMES, ROWS, COLS, CH), 1.0, 6.0, ((0, 2), (1, 8), (2, 2))),
        "w_spatial": bell_draw(arg_keys[2], (3, 3, CH, CH), (9 * CH) ** -0.5, 0.125),
        "w_temporal": bell_draw(arg_keys[3], (3, CH, CH), (3 * CH) ** -0.5, 0.21875),
    }


def silu_slope(values):
    sigmoid_value = jax.nn.sigmoid(values)
    return sigmoid_value * (1.0 + values * (1.0 - sigmoid_value))

def forward_taps(padded, row_count, col_count):
    pieces = [padded[row_tap:row_tap + row_count, col_tap:col_tap + col_count] for row_tap in range(3) for col_tap in range(3)]
    return jnp.concatenate(pieces, axis=-1)

def backward_taps(padded, row_count, col_count):
    pieces = [padded[2 - row_tap:2 - row_tap + row_count, 2 - col_tap:2 - col_tap + col_count] for row_tap in range(3) for col_tap in range(3)]
    return jnp.concatenate(pieces, axis=-1)

def reference(frames_in, cotangent, w_spatial, w_temporal):
    channels = w_temporal.shape[-1]
    spatial_flat = w_spatial.reshape(9 * channels, channels)
    temporal_flat = w_temporal.reshape(3 * channels, channels)
    spatial_back = jnp.concatenate([w_spatial[row_tap, col_tap].T for row_tap in range(3) for col_tap in range(3)], axis=0)
    temporal_back = jnp.concatenate([w_temporal[2].T, w_temporal[1].T, w_temporal[0].T], axis=0)
    contract = (((0,), (0,)), ((), ()))

    def one_clip(operands):
        inputs, upstream = operands
        activated = jax.nn.silu(inputs.astype(jnp.float32)).astype(jnp.bfloat16)

        def spatial_frame(frame):
            padded = jnp.pad(frame, ((1, 1), (1, 1), (0, 0)))
            stacked = forward_taps(padded, ROWS, COLS).reshape(-1, 9 * channels)
            product = jnp.dot(stacked, spatial_flat, preferred_element_type=jnp.float32)
            return product.astype(jnp.bfloat16).reshape(ROWS, COLS, channels)
        spatial_out = lax.map(spatial_frame, activated)
        padded_frames = jnp.concatenate([spatial_out[:1], spatial_out[:1], spatial_out], axis=0)
        upstream_ext = jnp.concatenate([upstream, jnp.zeros((2, ROWS, COLS, channels), jnp.bfloat16)], axis=0)

        def temporal_frame(index):
            slab = lax.dynamic_slice_in_dim(padded_frames, index, 3, 0)
            stacked = jnp.concatenate([slab[0], slab[1], slab[2]], axis=-1).reshape(-1, 3 * channels)
            grad_slab = lax.dynamic_slice_in_dim(upstream_ext, index, 3, 0)
            grad_stack = jnp.concatenate([grad_slab[0], grad_slab[1], grad_slab[2]], axis=-1).reshape(-1, 3 * channels)
            forward_part = jnp.dot(stacked, temporal_flat, preferred_element_type=jnp.float32)
            backward_part = jnp.dot(grad_stack, temporal_back, preferred_element_type=jnp.float32)
            return (forward_part.reshape(ROWS, COLS, channels), backward_part.reshape(ROWS, COLS, channels))
        frame_index = jnp.arange(FRAMES, dtype=jnp.int32)
        temporal_out, frame_sum = lax.map(temporal_frame, frame_index)
        first_up = upstream[0].reshape(-1, channels)
        second_up = upstream[1].reshape(-1, channels)
        fold_term = jnp.dot(first_up, w_temporal[0].T, preferred_element_type=jnp.float32)
        fold_term = fold_term + jnp.dot(first_up, w_temporal[1].T, preferred_element_type=jnp.float32)
        fold_term = fold_term + jnp.dot(second_up, w_temporal[0].T, preferred_element_type=jnp.float32)
        frame_sum = frame_sum.at[0].add(fold_term.reshape(ROWS, COLS, channels))
        frame_grad = frame_sum.astype(jnp.bfloat16)
        decoded = (inputs.astype(jnp.float32) + temporal_out).astype(jnp.bfloat16)

        def back_frame(frame):
            padded = jnp.pad(frame, ((1, 1), (1, 1), (0, 0)))
            stacked = backward_taps(padded, ROWS, COLS).reshape(-1, 9 * channels)
            return jnp.dot(stacked, spatial_back, preferred_element_type=jnp.float32).reshape(ROWS, COLS, channels)
        act_grad = lax.map(back_frame, frame_grad)
        input_grad = (upstream.astype(jnp.float32) + silu_slope(inputs.astype(jnp.float32)) * act_grad).astype(jnp.bfloat16)

        def accumulate(carry, index):
            spatial_acc, temporal_acc = carry
            frame = lax.dynamic_index_in_dim(activated, index, 0, keepdims=False)
            padded = jnp.pad(frame, ((1, 1), (1, 1), (0, 0)))
            stacked = forward_taps(padded, ROWS, COLS).reshape(-1, 9 * channels)
            grad_frame = lax.dynamic_index_in_dim(frame_grad, index, 0, keepdims=False).reshape(-1, channels)
            spatial_acc = spatial_acc + lax.dot_general(stacked, grad_frame, contract, preferred_element_type=jnp.float32)
            slab = lax.dynamic_slice_in_dim(padded_frames, index, 3, 0)
            frame_stack = jnp.concatenate([slab[0], slab[1], slab[2]], axis=-1).reshape(-1, 3 * channels)
            up_frame = lax.dynamic_index_in_dim(upstream, index, 0, keepdims=False).reshape(-1, channels)
            temporal_acc = temporal_acc + lax.dot_general(frame_stack, up_frame, contract, preferred_element_type=jnp.float32)
            return ((spatial_acc, temporal_acc), None)
        start = (jnp.zeros((9 * channels, channels), jnp.float32), jnp.zeros((3 * channels, channels), jnp.float32))
        (spatial_acc, temporal_acc), unused = lax.scan(accumulate, start, frame_index)
        return (decoded, input_grad, spatial_acc, temporal_acc)
    decoded, input_grad, spatial_sums, temporal_sums = lax.map(one_clip, (frames_in, cotangent))
    grad_scale = 1.0 / math.sqrt(CELLS)
    spatial_grad = (lax.optimization_barrier(jnp.sum(spatial_sums, axis=0)) * grad_scale).astype(jnp.bfloat16).reshape(3, 3, channels, channels)
    temporal_grad = (lax.optimization_barrier(jnp.sum(temporal_sums, axis=0)) * grad_scale).astype(jnp.bfloat16).reshape(3, channels, channels)
    return (decoded, input_grad, spatial_grad, temporal_grad)
```

```python
import functools
import math

import jax
import jax.numpy as jnp
from jax import lax
from jax.experimental import pallas as pl
from jax.experimental.pallas import tpu as pltpu
from jax.sharding import PartitionSpec as P

F32 = jnp.float32
BF16 = jnp.bfloat16
GROUPS = 3


def split_bit(axis, distance):
    index = lax.axis_index(axis)
    bit = lax.rem(lax.div(index, distance), 2)
    return bit, index + distance - 2 * distance * bit


def plans(sizes):
    near = [("tm", 1), ("height", 1), ("tm", 2)]
    rest = [
        (axis, 1 << b)
        for axis in ("tm", "height")
        for b in range(sizes[axis].bit_length() - 1)
        if (axis, 1 << b) not in near
    ]
    result = []
    for g in range(GROUPS):
        order = [("dp", 1)] + near[g:] + near[:g]
        result.append([(a, d, True) for a, d in order] + [(a, d, False) for a, d in rest])
    return result


def sums_layout(plan, rows):
    spots, at, size = [], 0, rows
    for _, _, halves in plan:
        size = size // 2 if halves else size
        spots.append((at, size))
        at += size
    return spots, at


def sigmoid(v):
    return 1.0 / (1.0 + jnp.exp(-v))


def shifted(v, cols):
    cells, ch = v.shape
    col = lax.broadcasted_iota(jnp.int32, (cells // cols, cols, ch), 1).reshape(cells, ch)
    before = jnp.where(col == 0, 0.0, pltpu.roll(v, 1, 0))
    after = jnp.where(col == cols - 1, 0.0, pltpu.roll(v, cells - 1, 0))
    return before, after


def dot_nn(a, b):
    return jnp.dot(a, b, preferred_element_type=F32)


def dot_nt(a, b):
    return lax.dot_general(a, b, (((1,), (1,)), ((), ())), preferred_element_type=F32)


def dot_tn(a, b):
    return lax.dot_general(a, b, (((0,), (0,)), ((), ())), preferred_element_type=F32)


def kernel(
    sizes, scale,
    x_ref, c_ref, ws_ref, wt_ref,
    dec_ref, ig_ref, sg_ref, tg_ref,
    xh, ch, soh, fgh, so, fg, s_buf, t_buf, acc, sb, rb, full,
    halo_send, halo_recv, sum_send, sum_recv,
):
    frames, rows, cols, chan = x_ref.shape
    cells = frames * rows * cols
    tm, height = lax.axis_index("tm"), lax.axis_index("height")
    n_tm, n_h = sizes["tm"], sizes["height"]
    group_plans = plans(sizes)
    group_rows = 12 * chan // GROUPS
    spots, _ = sums_layout(group_plans[0], group_rows)

    has_prev, has_next = tm > 0, tm < n_tm - 1
    has_up, has_down = height > 0, height < n_h - 1

    barrier = pltpu.get_barrier_semaphore()

    def greet(device):
        pl.semaphore_signal(barrier, inc=1, device_id=device, device_id_type=pl.DeviceIdType.MESH)

    bits = sorted({(a, d) for a, d, _ in group_plans[0]})
    for axis, distance in bits:
        greet({axis: split_bit(axis, distance)[1]})
    pl.when(has_prev)(lambda: greet({"tm": tm - 1}))
    pl.when(has_next)(lambda: greet({"tm": tm + 1}))
    pl.when(has_up)(lambda: greet({"height": height - 1}))
    pl.when(has_down)(lambda: greet({"height": height + 1}))
    expected = len(bits) + sum(
        jnp.where(has, 1, 0) for has in (has_prev, has_next, has_up, has_down)
    )
    pl.semaphore_wait(barrier, expected)

    def remote(src, dst, sems, device):
        return pltpu.make_async_remote_copy(
            src_ref=src, dst_ref=dst, send_sem=sems[0], recv_sem=sems[1],
            device_id=device, device_id_type=pl.DeviceIdType.MESH,
        )

    def halo(at):
        return halo_send.at[at], halo_recv.at[at]

    x_up = remote(x_ref.at[:, 0], xh.at[1], halo(0), {"height": height - 1})
    x_down = remote(x_ref.at[:, rows - 1], xh.at[0], halo(1), {"height": height + 1})
    c_prev = remote(c_ref.at[pl.ds(0, 2)], ch, halo(2), {"tm": tm - 1})
    so_next = remote(so.at[pl.ds(frames - 2, 2)], soh, halo(3), {"tm": tm + 1})
    fg_up = remote(fg.at[:, 0], fgh.at[1], halo(4), {"height": height - 1})
    fg_down = remote(fg.at[:, rows - 1], fgh.at[0], halo(5), {"height": height + 1})

    pl.when(has_prev)(c_prev.start)
    pl.when(has_up)(x_up.start)
    pl.when(has_down)(x_down.start)

    def taps(buf, part, value, count, flip):
        value = value.reshape(-1, chan)
        before, after = shifted(value, cols)
        if flip:
            before, after = after, before
        for j, v in enumerate((before, value, after)):
            v = v.astype(BF16).reshape(frames, count, cols, chan)
            buf[:, part : part + count, :, j * chan : (j + 1) * chan] = v

    def activation(v):
        v = v.astype(F32)
        return (v * sigmoid(v)).astype(BF16).astype(F32)

    taps(s_buf, 1, activation(x_ref[...]), rows, False)

    @pl.when(has_up)
    def _():
        x_down.wait_recv()

    @pl.when(jnp.logical_not(has_up))
    def _():
        xh[0] = jnp.zeros((frames, cols, chan), BF16)

    @pl.when(has_down)
    def _():
        x_up.wait_recv()

    @pl.when(jnp.logical_not(has_down))
    def _():
        xh[1] = jnp.zeros((frames, cols, chan), BF16)

    taps(s_buf, 0, activation(xh[0]), 1, False)
    taps(s_buf, rows + 1, activation(xh[1]), 1, False)

    def s_rows(i):
        return s_buf[:, i : i + rows].reshape(cells, 3 * chan)

    out = dot_nn(s_rows(0), ws_ref[0])
    out += dot_nn(s_rows(1), ws_ref[1])
    out += dot_nn(s_rows(2), ws_ref[2])
    so[...] = out.astype(BF16).reshape(frames, rows, cols, chan)
    pl.when(has_next)(so_next.start)

    @pl.when(has_next)
    def _():
        c_prev.wait_recv()

    @pl.when(jnp.logical_not(has_next))
    def _():
        ch[...] = jnp.zeros(ch.shape, BF16)

    def later(offset):
        if offset == 0:
            return c_ref[...].reshape(cells, chan)
        parts = [c_ref[offset:], ch[:offset]]
        return jnp.concatenate(parts, axis=0).reshape(cells, chan)

    fg_sum = dot_nt(later(0), wt_ref[2])
    fg_sum += dot_nt(later(1), wt_ref[1])
    fg_sum += dot_nt(later(2), wt_ref[0])
    fg[...] = fg_sum.astype(BF16).reshape(frames, rows, cols, chan)

    @pl.when(tm == 0)
    def _():
        c0 = c_ref[0].reshape(-1, chan)
        c1 = c_ref[1].reshape(-1, chan)
        fold = dot_nt(c0, wt_ref[0]) + dot_nt(c0, wt_ref[1]) + dot_nt(c1, wt_ref[0])
        fg[0] = (fg_sum[: rows * cols] + fold).astype(BF16).reshape(rows, cols, chan)

    pl.when(has_up)(fg_up.start)
    pl.when(has_down)(fg_down.start)

    def tap_term(tap):
        if tap < 9:
            i, j = tap // 3, tap % 3
            left = s_buf[:, i : i + rows, :, j * chan : (j + 1) * chan].reshape(cells, chan)
            return dot_tn(left, fg[...].reshape(cells, chan))
        return dot_tn(so[...].reshape(cells, chan), later(2 - (tap - 9)))

    def sum_copy(g, step):
        axis, distance, _ = group_plans[g][step]
        at, size = spots[step]
        place = (g, pl.ds(at, size))
        sems = (sum_send.at[g, step], sum_recv.at[g, step])
        return remote(sb.at[place], rb.at[place], sems, {axis: split_bit(axis, distance)[1]})

    steps = len(group_plans[0])
    halvings = sum(halves for _, _, halves in group_plans[0])
    firsts = [[] for _ in range(GROUPS)]

    def piece(start, size):
        return pl.ds(pl.multiple_of(start, size), size)

    def begin(g):
        bit, _ = split_bit(*group_plans[g][0][:2])
        at, size = spots[0]
        sb[g, at : at + size] = acc[g, piece((1 - bit) * size, size)].astype(BF16)
        sum_copy(g, 0).start()
        firsts[g].append(bit * size)

    def advance(g, step):
        sum_copy(g, step).wait_recv()
        at, size = spots[step]
        halved = group_plans[g][step][2]
        first = firsts[g][-1]
        last = step == steps - 1
        if not last and group_plans[g][step + 1][2]:
            bit, _ = split_bit(*group_plans[g][step + 1][:2])
            next_at, half = spots[step + 1]
            away, kept = (1 - bit) * half, bit * half
            total = acc[g, piece(first + away, half)] + rb[g, piece(at + away, half)].astype(F32)
            sb[g, next_at : next_at + half] = total.astype(BF16)
            sum_copy(g, step + 1).start()
            acc[g, piece(first + kept, half)] += rb[g, piece(at + kept, half)].astype(F32)
            firsts[g].append(first + kept)
            return
        mine = acc[g, piece(first, size)] if halved else sb[g, at : at + size].astype(F32)
        total = (mine + rb[g, at : at + size].astype(F32)).astype(BF16)
        if last:
            full[g, piece(first, size)] = total
            spread(g, halvings - 1).start()
        else:
            next_at, _ = spots[step + 1]
            sb[g, next_at : next_at + size] = total
            sum_copy(g, step + 1).start()

    def spread(g, level):
        axis, distance, _ = group_plans[g][level]
        size = spots[level][1]
        place = full.at[g, piece(firsts[g][level], size)]
        sems = (sum_send.at[g, steps + level], sum_recv.at[g, steps + level])
        return remote(place, place, sems, {axis: split_bit(axis, distance)[1]})

    for g in range(GROUPS):
        for t in range(4):
            acc[g, t * chan : (t + 1) * chan] = tap_term(4 * g + t) * scale
        if g == GROUPS - 1:

            @pl.when(tm == 0)
            def _():
                so0 = so[0].reshape(-1, chan)
                c0 = c_ref[0].reshape(-1, chan)
                c1 = c_ref[1].reshape(-1, chan)
                once = dot_tn(so0, c0) * scale
                acc[g, chan : 2 * chan] += once + dot_tn(so0, c1) * scale
                acc[g, 2 * chan : 3 * chan] += once

        begin(g)

    def make_decoded():
        @pl.when(has_prev)
        def _():
            so_next.wait_recv()

        @pl.when(jnp.logical_not(has_prev))
        def _():
            soh[0] = so[0]
            soh[1] = so[0]

        def earlier(back):
            if back == 0:
                return so[...].reshape(cells, chan)
            parts = [soh[2 - back :], so[: frames - back]]
            return jnp.concatenate(parts, axis=0).reshape(cells, chan)

        total = dot_nn(earlier(0), wt_ref[2])
        total += dot_nn(earlier(1), wt_ref[1])
        total += dot_nn(earlier(2), wt_ref[0])
        total += x_ref[...].astype(F32).reshape(cells, chan)
        dec_ref[...] = total.astype(BF16).reshape(frames, rows, cols, chan)

    def make_grad_taps():
        taps(t_buf, 1, fg[...].astype(F32), rows, True)

        @pl.when(has_up)
        def _():
            fg_down.wait_recv()

        @pl.when(jnp.logical_not(has_up))
        def _():
            fgh[0] = jnp.zeros((frames, cols, chan), BF16)

        @pl.when(has_down)
        def _():
            fg_up.wait_recv()

        @pl.when(jnp.logical_not(has_down))
        def _():
            fgh[1] = jnp.zeros((frames, cols, chan), BF16)

        taps(t_buf, 0, fgh[0].astype(F32), 1, True)
        taps(t_buf, rows + 1, fgh[1].astype(F32), 1, True)

    def make_input_grad():
        total = None
        for i in range(3):
            for j in range(3):
                left = t_buf[:, 2 - i : 2 - i + rows, :, j * chan : (j + 1) * chan]
                term = dot_nt(
                    left.reshape(cells, chan), ws_ref[i, j * chan : (j + 1) * chan]
                )
                total = term if total is None else total + term
        x = x_ref[...].astype(F32).reshape(cells, chan)
        s = sigmoid(x)
        grad = c_ref[...].astype(F32).reshape(cells, chan) + s * (1.0 + x * (1.0 - s)) * total
        ig_ref[...] = grad.astype(BF16).reshape(frames, rows, cols, chan)

    work = [None, make_decoded, make_grad_taps, None]
    for step in range(steps):
        for g in range(GROUPS):
            advance(g, step)
        if step < len(work) and work[step] is not None:
            work[step]()
        if step == steps - 2:
            make_input_grad()
    for level in reversed(range(halvings)):
        for g in range(GROUPS):
            spread(g, level).wait_recv()
            if level > 0:
                spread(g, level - 1).start()

    flat = full[...].reshape(12 * chan, chan)
    sg_ref[...] = flat[: 9 * chan]
    tg_ref[...] = flat[9 * chan :]

    pl.when(has_prev)(c_prev.wait_send)
    pl.when(has_next)(so_next.wait_send)
    for up, down in ((x_up, x_down), (fg_up, fg_down)):
        pl.when(has_up)(up.wait_send)
        pl.when(has_down)(down.wait_send)
    for g in range(GROUPS):
        for step in range(steps):
            sum_copy(g, step).wait_send()
        for level in range(halvings):
            spread(g, level).wait_send()


def local(sizes, frames_in, cotangent, w_spatial, w_temporal):
    x, c = frames_in[0], cotangent[0]
    frames, rows, cols, chan = x.shape
    cell_count = frames * rows * cols * sizes["tm"] * sizes["height"] * sizes["dp"]
    plan = plans(sizes)[0]
    group_rows = 12 * chan // GROUPS
    _, buffer_rows = sums_layout(plan, group_rows)
    exchanges = len(plan) + sum(halves for _, _, halves in plan)
    block = jax.ShapeDtypeStruct(x.shape, BF16)
    vmem = pl.BlockSpec(memory_space=pltpu.VMEM)
    decoded, input_grad, spatial, temporal = pl.pallas_call(
        functools.partial(kernel, sizes, 1.0 / math.sqrt(cell_count)),
        out_shape=(
            block,
            block,
            jax.ShapeDtypeStruct((9 * chan, chan), BF16),
            jax.ShapeDtypeStruct((3 * chan, chan), BF16),
        ),
        in_specs=[vmem] * 4,
        out_specs=(vmem,) * 4,
        scratch_shapes=[
            pltpu.VMEM((2, frames, cols, chan), BF16),
            pltpu.VMEM((2, rows, cols, chan), BF16),
            pltpu.VMEM((2, rows, cols, chan), BF16),
            pltpu.VMEM((2, frames, cols, chan), BF16),
            pltpu.VMEM(x.shape, BF16),
            pltpu.VMEM(x.shape, BF16),
            pltpu.VMEM((frames, rows + 2, cols, 3 * chan), BF16),
            pltpu.VMEM((frames, rows + 2, cols, 3 * chan), BF16),
            pltpu.VMEM((GROUPS, group_rows, chan), F32),
            pltpu.VMEM((GROUPS, buffer_rows, chan), BF16),
            pltpu.VMEM((GROUPS, buffer_rows, chan), BF16),
            pltpu.VMEM((GROUPS, group_rows, chan), BF16),
            pltpu.SemaphoreType.DMA((6,)),
            pltpu.SemaphoreType.DMA((6,)),
            pltpu.SemaphoreType.DMA((GROUPS, exchanges)),
            pltpu.SemaphoreType.DMA((GROUPS, exchanges)),
        ],
        compiler_params=pltpu.CompilerParams(
            collective_id=0, has_side_effects=True, vmem_limit_bytes=48 * 1024 * 1024
        ),
    )(x, c, w_spatial.reshape(3, 3 * chan, chan), w_temporal)
    return (
        decoded[None],
        input_grad[None],
        spatial.reshape(3, 3, chan, chan),
        temporal.reshape(3, chan, chan),
    )


def solution(mesh):
    sizes = dict(mesh.shape)
    spec = P("dp", "tm", "height", None, None)
    return jax.shard_map(
        functools.partial(local, sizes),
        mesh=mesh,
        in_specs=(spec, spec, P(), P()),
        out_specs=(spec, spec, P(), P()),
        check_vma=False,
    )
```

```python
import functools
import math

import jax
import jax.numpy as jnp
from jax import lax
from jax.experimental import pallas as pl
from jax.experimental.pallas import tpu as pltpu
from jax.sharding import PartitionSpec as P

F32 = jnp.float32
BF16 = jnp.bfloat16
GROUPS = 6
VMEM_LIMIT = 60 * 1024 * 1024


def split_bit(axis, distance):
    index = lax.axis_index(axis)
    bit = lax.rem(lax.div(index, distance), 2)
    return bit, index + distance - 2 * distance * bit


def plans(sizes):
    near = [("tm", 1), ("height", 1), ("tm", 2)]
    rest = [
        (axis, 1 << b)
        for axis in ("tm", "height")
        for b in range(sizes[axis].bit_length() - 1)
        if (axis, 1 << b) not in near
    ]
    result = []
    for g in range(GROUPS):
        turn = g % len(near)
        order = [("dp", 1)] + near[turn:] + near[:turn]
        result.append([(a, d, True) for a, d in order] + [(a, d, False) for a, d in rest])
    return result


def sums_layout(plan, rows):
    spots, at, size = [], 0, rows
    for _, _, halves in plan:
        size = size // 2 if halves else size
        spots.append((at, size))
        at += size
    return spots, at


def sigmoid(v):
    return 1.0 / (1.0 + jnp.exp(-v))


def shifted(v, cols):
    cells, ch = v.shape
    col = lax.broadcasted_iota(jnp.int32, (cells // cols, cols, ch), 1).reshape(cells, ch)
    before = jnp.where(col == 0, 0.0, pltpu.roll(v, 1, 0))
    after = jnp.where(col == cols - 1, 0.0, pltpu.roll(v, cells - 1, 0))
    return before, after


def dot_nn(a, b):
    return jnp.dot(a, b, preferred_element_type=F32)


def dot_nt(a, b):
    return lax.dot_general(a, b, (((1,), (1,)), ((), ())), preferred_element_type=F32)


def dot_tn(a, b):
    return lax.dot_general(a, b, (((0,), (0,)), ((), ())), preferred_element_type=F32)


def kernel(
    sizes, scale,
    x_hbm, c_hbm, ws_hbm, wt_hbm,
    dec_hbm, ig_hbm, sg_hbm, tg_hbm,
    dec_ref, ig_ref,    x_ref, c_ref, ws_ref, wt_ref, xh, ch, soh, fgh, so, fg, s_buf, t_buf, acc, sb, rb, full,
    load_sem, store_sem, halo_send, halo_recv, sum_send, sum_recv,
):
    frames, rows, cols, chan = x_ref.shape
    cells = frames * rows * cols
    tm, height = lax.axis_index("tm"), lax.axis_index("height")
    n_tm, n_h = sizes["tm"], sizes["height"]
    group_plans = plans(sizes)
    per_group = 12 // GROUPS
    group_rows = per_group * chan
    spots, _ = sums_layout(group_plans[0], group_rows)

    has_prev, has_next = tm > 0, tm < n_tm - 1
    has_up, has_down = height > 0, height < n_h - 1

    loads = [
        pltpu.make_async_copy(src, dst, load_sem.at[n])
        for n, (src, dst) in enumerate(
            ((x_hbm, x_ref), (ws_hbm, ws_ref), (c_hbm, c_ref), (wt_hbm, wt_ref))
        )
    ]
    for load in loads:
        load.start()

    barrier = pltpu.get_barrier_semaphore()

    def greet(device):
        pl.semaphore_signal(barrier, inc=1, device_id=device, device_id_type=pl.DeviceIdType.MESH)

    bits = sorted({(a, d) for a, d, _ in group_plans[0]})
    for axis, distance in bits:
        greet({axis: split_bit(axis, distance)[1]})
    pl.when(has_prev)(lambda: greet({"tm": tm - 1}))
    pl.when(has_next)(lambda: greet({"tm": tm + 1}))
    pl.when(has_up)(lambda: greet({"height": height - 1}))
    pl.when(has_down)(lambda: greet({"height": height + 1}))
    expected = len(bits) + sum(
        jnp.where(has, 1, 0) for has in (has_prev, has_next, has_up, has_down)
    )
    pl.semaphore_wait(barrier, expected)

    def remote(src, dst, sems, device):
        return pltpu.make_async_remote_copy(
            src_ref=src, dst_ref=dst, send_sem=sems[0], recv_sem=sems[1],
            device_id=device, device_id_type=pl.DeviceIdType.MESH,
        )

    def halo(at):
        return halo_send.at[at], halo_recv.at[at]

    x_up = remote(x_hbm.at[:, 0], xh.at[1], halo(0), {"height": height - 1})
    x_down = remote(x_hbm.at[:, rows - 1], xh.at[0], halo(1), {"height": height + 1})
    c_prev = remote(c_hbm.at[pl.ds(0, 2)], ch, halo(2), {"tm": tm - 1})
    so_next = remote(so.at[pl.ds(frames - 2, 2)], soh, halo(3), {"tm": tm + 1})
    fg_up = remote(fg.at[:, 0], fgh.at[1], halo(4), {"height": height - 1})
    fg_down = remote(fg.at[:, rows - 1], fgh.at[0], halo(5), {"height": height + 1})

    pl.when(has_prev)(c_prev.start)
    pl.when(has_up)(x_up.start)
    pl.when(has_down)(x_down.start)

    def taps(buf, part, value, count, flip):
        value = value.reshape(-1, chan)
        before, after = shifted(value, cols)
        if flip:
            before, after = after, before
        for j, v in enumerate((before, value, after)):
            v = v.astype(BF16).reshape(frames, count, cols, chan)
            buf[:, part : part + count, :, j * chan : (j + 1) * chan] = v

    def activation(v):
        v = v.astype(F32)
        return (v * sigmoid(v)).astype(BF16).astype(F32)

    loads[0].wait()
    taps(s_buf, 1, activation(x_ref[...]), rows, False)
    for load in loads[1:]:
        load.wait()

    @pl.when(has_up)
    def _():
        x_down.wait_recv()

    @pl.when(jnp.logical_not(has_up))
    def _():
        xh[0] = jnp.zeros((frames, cols, chan), BF16)

    @pl.when(has_down)
    def _():
        x_up.wait_recv()

    @pl.when(jnp.logical_not(has_down))
    def _():
        xh[1] = jnp.zeros((frames, cols, chan), BF16)

    taps(s_buf, 0, activation(xh[0]), 1, False)
    taps(s_buf, rows + 1, activation(xh[1]), 1, False)

    def s_rows(i):
        return s_buf[:, i : i + rows].reshape(cells, 3 * chan)

    out = dot_nn(s_rows(0), ws_ref[0])
    out += dot_nn(s_rows(1), ws_ref[1])
    out += dot_nn(s_rows(2), ws_ref[2])
    so[...] = out.astype(BF16).reshape(frames, rows, cols, chan)
    pl.when(has_next)(so_next.start)

    @pl.when(has_next)
    def _():
        c_prev.wait_recv()

    @pl.when(jnp.logical_not(has_next))
    def _():
        ch[...] = jnp.zeros(ch.shape, BF16)

    def later(offset):
        if offset == 0:
            return c_ref[...].reshape(cells, chan)
        parts = [c_ref[offset:], ch[:offset]]
        return jnp.concatenate(parts, axis=0).reshape(cells, chan)

    fg_sum = dot_nt(later(0), wt_ref[2])
    fg_sum += dot_nt(later(1), wt_ref[1])
    fg_sum += dot_nt(later(2), wt_ref[0])
    fg[...] = fg_sum.astype(BF16).reshape(frames, rows, cols, chan)

    @pl.when(tm == 0)
    def _():
        c0 = c_ref[0].reshape(-1, chan)
        c1 = c_ref[1].reshape(-1, chan)
        fold = dot_nt(c0, wt_ref[0]) + dot_nt(c0, wt_ref[1]) + dot_nt(c1, wt_ref[0])
        fg[0] = (fg_sum[: rows * cols] + fold).astype(BF16).reshape(rows, cols, chan)

    pl.when(has_up)(fg_up.start)
    pl.when(has_down)(fg_down.start)

    def tap_term(tap):
        if tap < 9:
            i, j = tap // 3, tap % 3
            left = s_buf[:, i : i + rows, :, j * chan : (j + 1) * chan].reshape(cells, chan)
            return dot_tn(left, fg[...].reshape(cells, chan))
        return dot_tn(so[...].reshape(cells, chan), later(2 - (tap - 9)))

    def sum_copy(g, step):
        axis, distance, _ = group_plans[g][step]
        at, size = spots[step]
        place = (g, pl.ds(at, size))
        sems = (sum_send.at[g, step], sum_recv.at[g, step])
        return remote(sb.at[place], rb.at[place], sems, {axis: split_bit(axis, distance)[1]})

    steps = len(group_plans[0])
    halvings = sum(halves for _, _, halves in group_plans[0])
    firsts = [[] for _ in range(GROUPS)]

    def piece(start, size):
        return pl.ds(pl.multiple_of(start, size), size)

    def begin(g):
        bit, _ = split_bit(*group_plans[g][0][:2])
        at, size = spots[0]
        sb[g, at : at + size] = acc[g, piece((1 - bit) * size, size)].astype(BF16)
        sum_copy(g, 0).start()
        firsts[g].append(bit * size)

    def advance(g, step):
        sum_copy(g, step).wait_recv()
        at, size = spots[step]
        halved = group_plans[g][step][2]
        first = firsts[g][-1]
        last = step == steps - 1
        if not last and group_plans[g][step + 1][2]:
            bit, _ = split_bit(*group_plans[g][step + 1][:2])
            next_at, half = spots[step + 1]
            away, kept = (1 - bit) * half, bit * half
            total = acc[g, piece(first + away, half)] + rb[g, piece(at + away, half)].astype(F32)
            sb[g, next_at : next_at + half] = total.astype(BF16)
            sum_copy(g, step + 1).start()
            acc[g, piece(first + kept, half)] += rb[g, piece(at + kept, half)].astype(F32)
            firsts[g].append(first + kept)
            return
        mine = acc[g, piece(first, size)] if halved else sb[g, at : at + size].astype(F32)
        total = (mine + rb[g, at : at + size].astype(F32)).astype(BF16)
        if last:
            full[g, piece(first, size)] = total
            spread(g, halvings - 1).start()
        else:
            next_at, _ = spots[step + 1]
            sb[g, next_at : next_at + size] = total
            sum_copy(g, step + 1).start()

    def spread(g, level):
        axis, distance, _ = group_plans[g][level]
        size = spots[level][1]
        place = full.at[g, piece(firsts[g][level], size)]
        sems = (sum_send.at[g, steps + level], sum_recv.at[g, steps + level])
        return remote(place, place, sems, {axis: split_bit(axis, distance)[1]})

    for g in range(GROUPS):
        for t in range(per_group):
            tap = per_group * g + t
            acc[g, t * chan : (t + 1) * chan] = tap_term(tap) * scale
            if tap in (9, 10):

                @pl.when(tm == 0)
                def _():
                    so0 = so[0].reshape(-1, chan)
                    extra = dot_tn(so0, c_ref[0].reshape(-1, chan))
                    if tap == 9:
                        extra += dot_tn(so0, c_ref[1].reshape(-1, chan))
                    acc[g, t * chan : (t + 1) * chan] += extra * scale

        begin(g)

    store_dec = pltpu.make_async_copy(dec_ref, dec_hbm, store_sem.at[0])
    store_ig = pltpu.make_async_copy(ig_ref, ig_hbm, store_sem.at[1])

    def store_tap(tap):
        g, t = tap // per_group, tap % per_group
        to = sg_hbm.at[tap] if tap < 9 else tg_hbm.at[tap - 9]
        return pltpu.make_async_copy(
            full.at[g, t * chan : (t + 1) * chan], to, store_sem.at[2 + tap]
        )

    def make_decoded():
        @pl.when(has_prev)
        def _():
            so_next.wait_recv()

        @pl.when(jnp.logical_not(has_prev))
        def _():
            soh[0] = so[0]
            soh[1] = so[0]

        def earlier(back):
            if back == 0:
                return so[...].reshape(cells, chan)
            parts = [soh[2 - back :], so[: frames - back]]
            return jnp.concatenate(parts, axis=0).reshape(cells, chan)

        total = dot_nn(earlier(0), wt_ref[2])
        total += dot_nn(earlier(1), wt_ref[1])
        total += dot_nn(earlier(2), wt_ref[0])
        total += x_ref[...].astype(F32).reshape(cells, chan)
        dec_ref[...] = total.astype(BF16).reshape(frames, rows, cols, chan)
        store_dec.start()

    def make_grad_taps():
        taps(t_buf, 1, fg[...].astype(F32), rows, True)

        @pl.when(has_up)
        def _():
            fg_down.wait_recv()

        @pl.when(jnp.logical_not(has_up))
        def _():
            fgh[0] = jnp.zeros((frames, cols, chan), BF16)

        @pl.when(has_down)
        def _():
            fg_up.wait_recv()

        @pl.when(jnp.logical_not(has_down))
        def _():
            fgh[1] = jnp.zeros((frames, cols, chan), BF16)

        taps(t_buf, 0, fgh[0].astype(F32), 1, True)
        taps(t_buf, rows + 1, fgh[1].astype(F32), 1, True)

    def make_input_grad():
        total = None
        for i in range(3):
            for j in range(3):
                left = t_buf[:, 2 - i : 2 - i + rows, :, j * chan : (j + 1) * chan]
                term = dot_nt(
                    left.reshape(cells, chan), ws_ref[i, j * chan : (j + 1) * chan]
                )
                total = term if total is None else total + term
        x = x_ref[...].astype(F32).reshape(cells, chan)
        s = sigmoid(x)
        grad = c_ref[...].astype(F32).reshape(cells, chan) + s * (1.0 + x * (1.0 - s)) * total
        ig_ref[...] = grad.astype(BF16).reshape(frames, rows, cols, chan)
        store_ig.start()

    work = [None, make_decoded, make_grad_taps, None]
    for step in range(steps):
        for g in range(GROUPS):
            advance(g, step)
        if step < len(work) and work[step] is not None:
            work[step]()
        if step == steps - 2:
            make_input_grad()
    for level in reversed(range(halvings)):
        for g in range(GROUPS):
            spread(g, level).wait_recv()
            if level > 0:
                spread(g, level - 1).start()
            else:
                for t in range(per_group):
                    store_tap(per_group * g + t).start()

    pl.when(has_prev)(c_prev.wait_send)
    pl.when(has_next)(so_next.wait_send)
    for up, down in ((x_up, x_down), (fg_up, fg_down)):
        pl.when(has_up)(up.wait_send)
        pl.when(has_down)(down.wait_send)
    for g in range(GROUPS):
        for step in range(steps):
            sum_copy(g, step).wait_send()
        for level in range(halvings):
            spread(g, level).wait_send()
    store_dec.wait()
    store_ig.wait()
    for tap in range(12):
        store_tap(tap).wait()


def write_out(dec_in, ig_in, sg_in, tg_in, dec_out, ig_out, sg_out, tg_out, sem):
    pairs = [(dec_in, dec_out), (ig_in, ig_out), (tg_in, tg_out)]
    pairs += [(sg_in.at[3 * i : 3 * i + 3], sg_out.at[3 * i : 3 * i + 3]) for i in range(3)]
    copies = [pltpu.make_async_copy(a, b, sem.at[n]) for n, (a, b) in enumerate(pairs)]
    for copy in copies:
        copy.start()
    for copy in copies:
        copy.wait()


def local(sizes, frames_in, cotangent, w_spatial, w_temporal):
    x, c = frames_in[0], cotangent[0]
    frames, rows, cols, chan = x.shape
    cell_count = frames * rows * cols * sizes["tm"] * sizes["height"] * sizes["dp"]
    plan = plans(sizes)[0]
    group_rows = 12 * chan // GROUPS
    _, buffer_rows = sums_layout(plan, group_rows)
    exchanges = len(plan) + sum(halves for _, _, halves in plan)
    block = jax.ShapeDtypeStruct(x.shape, BF16)
    hbm = pl.BlockSpec(memory_space=pltpu.HBM)
    results = pl.pallas_call(
        functools.partial(kernel, sizes, 1.0 / math.sqrt(cell_count)),
        out_shape=(
            block,
            block,
            jax.ShapeDtypeStruct((9, chan, chan), BF16),
            jax.ShapeDtypeStruct((3, chan, chan), BF16),
        ),
        in_specs=[hbm] * 4,
        out_specs=(hbm,) * 4,
        scratch_shapes=[
            pltpu.VMEM(x.shape, BF16),
            pltpu.VMEM(x.shape, BF16),
            pltpu.VMEM(x.shape, BF16),
            pltpu.VMEM(x.shape, BF16),
            pltpu.VMEM((3, 3 * chan, chan), BF16),
            pltpu.VMEM(w_temporal.shape, BF16),
            pltpu.VMEM((2, frames, cols, chan), BF16),
            pltpu.VMEM((2, rows, cols, chan), BF16),
            pltpu.VMEM((2, rows, cols, chan), BF16),
            pltpu.VMEM((2, frames, cols, chan), BF16),
            pltpu.VMEM(x.shape, BF16),
            pltpu.VMEM(x.shape, BF16),
            pltpu.VMEM((frames, rows + 2, cols, 3 * chan), BF16),
            pltpu.VMEM((frames, rows + 2, cols, 3 * chan), BF16),
            pltpu.VMEM((GROUPS, group_rows, chan), F32),
            pltpu.VMEM((GROUPS, buffer_rows, chan), BF16),
            pltpu.VMEM((GROUPS, buffer_rows, chan), BF16),
            pltpu.VMEM((GROUPS, group_rows, chan), BF16),
            pltpu.SemaphoreType.DMA((4,)),
            pltpu.SemaphoreType.DMA((14,)),
            pltpu.SemaphoreType.DMA((6,)),
            pltpu.SemaphoreType.DMA((6,)),
            pltpu.SemaphoreType.DMA((GROUPS, exchanges)),
            pltpu.SemaphoreType.DMA((GROUPS, exchanges)),
        ],
        compiler_params=pltpu.CompilerParams(
            collective_id=0, has_side_effects=True, vmem_limit_bytes=VMEM_LIMIT
        ),
    )(x, c, w_spatial.reshape(3, 3 * chan, chan), w_temporal)
    decoded, input_grad, spatial, temporal = pl.pallas_call(
        write_out,
        out_shape=tuple(jax.ShapeDtypeStruct(r.shape, r.dtype) for r in results),
        in_specs=[hbm] * 4,
        out_specs=(hbm,) * 4,
        scratch_shapes=[pltpu.SemaphoreType.DMA((6,))],
        compiler_params=pltpu.CompilerParams(vmem_limit_bytes=VMEM_LIMIT),
    )(*results)
    return (
        decoded[None],
        input_grad[None],
        spatial.reshape(3, 3, chan, chan),
        temporal.reshape(3, chan, chan),
    )


def solution(mesh):
    sizes = dict(mesh.shape)
    spec = P("dp", "tm", "height", None, None)
    return jax.shard_map(
        functools.partial(local, sizes),
        mesh=mesh,
        in_specs=(spec, spec, P(), P()),
        out_specs=(spec, spec, P(), P()),
        check_vma=False,
    )
```

```python
import functools
import math

import jax
import jax.numpy as jnp
from jax import lax
from jax.experimental import pallas as pl
from jax.experimental.pallas import tpu as pltpu
from jax.sharding import PartitionSpec as P

F32 = jnp.float32
BF16 = jnp.bfloat16
GROUPS = 6
VMEM_LIMIT = 60 * 1024 * 1024


def split_bit(axis, distance):
    return lax.rem(lax.div(lax.axis_index(axis), distance), 2)


def across(*flips):
    place = {}
    for axis, distance in flips:
        index = place.get(axis, lax.axis_index(axis))
        place[axis] = index + distance - 2 * distance * split_bit(axis, distance)
    return place


NEAR = (("tm", 1), ("height", 1), ("tm", 2))


def far_bits(sizes):
    return [
        (axis, 1 << b)
        for axis in ("tm", "height")
        for b in range(sizes[axis].bit_length() - 1)
        if (axis, 1 << b) not in NEAR
    ]


def near_order(g):
    turn = g % len(NEAR)
    return NEAR[turn:] + NEAR[:turn]


def sigmoid(v):
    return 1.0 / (1.0 + jnp.exp(-v))


def shifted(v, cols):
    cells, ch = v.shape
    col = lax.broadcasted_iota(jnp.int32, (cells // cols, cols, ch), 1).reshape(cells, ch)
    before = jnp.where(col == 0, 0.0, pltpu.roll(v, 1, 0))
    after = jnp.where(col == cols - 1, 0.0, pltpu.roll(v, cells - 1, 0))
    return before, after


def dot_nn(a, b):
    return jnp.dot(a, b, preferred_element_type=F32)


def dot_nt(a, b):
    return lax.dot_general(a, b, (((1,), (1,)), ((), ())), preferred_element_type=F32)


def dot_tn(a, b):
    return lax.dot_general(a, b, (((0,), (0,)), ((), ())), preferred_element_type=F32)


def kernel(
    sizes, scale,
    x_hbm, c_hbm, ws_hbm, wt_hbm,
    dec_hbm, ig_hbm, sg_hbm, tg_hbm,
    dec_ref, ig_ref,    x_ref, c_ref, ws_ref, wt_ref, xh, ch, soh, fgh, so, fg, s_buf, t_buf, acc, sb, rb, full,
    load_sem, store_sem, halo_send, halo_recv, sum_send, sum_recv,
):
    frames, rows, cols, chan = x_ref.shape
    cells = frames * rows * cols
    tm, height = lax.axis_index("tm"), lax.axis_index("height")
    n_tm, n_h = sizes["tm"], sizes["height"]
    far = far_bits(sizes)
    per_group = 12 // GROUPS
    group_rows = per_group * chan
    half, quarter, own = group_rows // 2, group_rows // 4, group_rows // 16

    has_prev, has_next = tm > 0, tm < n_tm - 1
    has_up, has_down = height > 0, height < n_h - 1

    loads = [
        pltpu.make_async_copy(src, dst, load_sem.at[n])
        for n, (src, dst) in enumerate(
            ((x_hbm, x_ref), (ws_hbm, ws_ref), (c_hbm, c_ref), (wt_hbm, wt_ref))
        )
    ]
    for load in loads:
        load.start()

    barrier = pltpu.get_barrier_semaphore()

    def greet(device):
        pl.semaphore_signal(barrier, inc=1, device_id=device, device_id_type=pl.DeviceIdType.MESH)

    pairs = [(NEAR[0], NEAR[1]), (NEAR[1], NEAR[2]), (NEAR[2], NEAR[0])]
    partners = [(bit,) for bit in ((("dp", 1),) + NEAR + tuple(far))] + pairs
    for flips in partners:
        greet(across(*flips))
    pl.when(has_prev)(lambda: greet({"tm": tm - 1}))
    pl.when(has_next)(lambda: greet({"tm": tm + 1}))
    pl.when(has_up)(lambda: greet({"height": height - 1}))
    pl.when(has_down)(lambda: greet({"height": height + 1}))
    expected = len(partners) + sum(
        jnp.where(has, 1, 0) for has in (has_prev, has_next, has_up, has_down)
    )
    pl.semaphore_wait(barrier, expected)

    def remote(src, dst, sems, device):
        return pltpu.make_async_remote_copy(
            src_ref=src, dst_ref=dst, send_sem=sems[0], recv_sem=sems[1],
            device_id=device, device_id_type=pl.DeviceIdType.MESH,
        )

    def halo(at):
        return halo_send.at[at], halo_recv.at[at]

    x_up = remote(x_hbm.at[:, 0], xh.at[1], halo(0), {"height": height - 1})
    x_down = remote(x_hbm.at[:, rows - 1], xh.at[0], halo(1), {"height": height + 1})
    c_prev = remote(c_hbm.at[pl.ds(0, 2)], ch, halo(2), {"tm": tm - 1})
    so_next = remote(so.at[pl.ds(frames - 2, 2)], soh, halo(3), {"tm": tm + 1})
    fg_up = remote(fg.at[:, 0], fgh.at[1], halo(4), {"height": height - 1})
    fg_down = remote(fg.at[:, rows - 1], fgh.at[0], halo(5), {"height": height + 1})

    pl.when(has_prev)(c_prev.start)
    pl.when(has_up)(x_up.start)
    pl.when(has_down)(x_down.start)

    def taps(buf, part, value, count, flip):
        value = value.reshape(-1, chan)
        before, after = shifted(value, cols)
        if flip:
            before, after = after, before
        for j, v in enumerate((before, value, after)):
            v = v.astype(BF16).reshape(frames, count, cols, chan)
            buf[:, part : part + count, :, j * chan : (j + 1) * chan] = v

    def activation(v):
        v = v.astype(F32)
        return (v * sigmoid(v)).astype(BF16).astype(F32)

    loads[0].wait()
    taps(s_buf, 1, activation(x_ref[...]), rows, False)
    for load in loads[1:]:
        load.wait()

    @pl.when(has_up)
    def _():
        x_down.wait_recv()

    @pl.when(jnp.logical_not(has_up))
    def _():
        xh[0] = jnp.zeros((frames, cols, chan), BF16)

    @pl.when(has_down)
    def _():
        x_up.wait_recv()

    @pl.when(jnp.logical_not(has_down))
    def _():
        xh[1] = jnp.zeros((frames, cols, chan), BF16)

    taps(s_buf, 0, activation(xh[0]), 1, False)
    taps(s_buf, rows + 1, activation(xh[1]), 1, False)

    def s_rows(i):
        return s_buf[:, i : i + rows].reshape(cells, 3 * chan)

    out = dot_nn(s_rows(0), ws_ref[0])
    out += dot_nn(s_rows(1), ws_ref[1])
    out += dot_nn(s_rows(2), ws_ref[2])
    so[...] = out.astype(BF16).reshape(frames, rows, cols, chan)
    pl.when(has_next)(so_next.start)

    def put_term(tap, term):
        g, t = tap // per_group, tap % per_group
        acc[g, t * chan : (t + 1) * chan] = term * scale
        if tap in (9, 10):

            @pl.when(tm == 0)
            def _():
                so0 = so[0].reshape(-1, chan)
                extra = dot_tn(so0, c_ref[0].reshape(-1, chan))
                if tap == 9:
                    extra += dot_tn(so0, c_ref[1].reshape(-1, chan))
                acc[g, t * chan : (t + 1) * chan] += extra * scale

    def temporal_term(tap):
        put_term(tap, dot_tn(so[...].reshape(cells, chan), later(2 - (tap - 9))))

    def spatial_term(tap):
        i, j = tap // 3, tap % 3
        left = s_buf[:, i : i + rows, :, j * chan : (j + 1) * chan].reshape(cells, chan)
        put_term(tap, dot_tn(left, fg[...].reshape(cells, chan)))

    def later(offset):
        if offset == 0:
            return c_ref[...].reshape(cells, chan)
        parts = [c_ref[offset:], ch[:offset]]
        return jnp.concatenate(parts, axis=0).reshape(cells, chan)

    temporal_term(11)

    @pl.when(has_next)
    def _():
        c_prev.wait_recv()

    @pl.when(jnp.logical_not(has_next))
    def _():
        ch[...] = jnp.zeros(ch.shape, BF16)

    def sum_copy(g, at, size, slot, flips):
        place = (g, pl.ds(at, size))
        sems = (sum_send.at[g, slot], sum_recv.at[g, slot])
        return remote(sb.at[place], rb.at[place], sems, across(*flips))

    def piece(start, size):
        return pl.ds(pl.multiple_of(start, size), size)

    def scatter_copies(g, step):
        first, second, third = near_order(g)
        if step == 0:
            return [sum_copy(g, 0, half, 0, [("dp", 1)])]
        if step == 1:
            return [sum_copy(g, half, quarter, 1, [first])]
        at = half + quarter
        if step == 2:
            return [
                sum_copy(g, at + n * own, own, 2 + n, flips)
                for n, flips in enumerate(([second], [third], [second, third]))
            ]
        return [sum_copy(g, at + step * own, own, 2 + step, [far[step - 3]])]

    steps = 3 + len(far)

    def kept(g):
        first, second, third = near_order(g)
        at_dp = split_bit("dp", 1) * half
        at_near = at_dp + split_bit(*first) * quarter
        return at_dp, at_near, at_near + (2 * split_bit(*second) + split_bit(*third)) * own

    def start_all(copies):
        for copy in copies:
            copy.start()

    def begin(g):
        sb[g, :half] = acc[g, piece((1 - split_bit("dp", 1)) * half, half)].astype(BF16)
        start_all(scatter_copies(g, 0))

    def advance(g, step):
        for copy in scatter_copies(g, step):
            copy.wait_recv()
        first, second, third = near_order(g)
        at_dp, at_near, at_own = kept(g)
        if step == 0:
            bit = split_bit(*first)
            away, stay = (1 - bit) * quarter, bit * quarter
            total = acc[g, piece(at_dp + away, quarter)] + rb[g, piece(away, quarter)].astype(F32)
            sb[g, half : half + quarter] = total.astype(BF16)
            start_all(scatter_copies(g, 1))
            acc[g, piece(at_dp + stay, quarter)] += rb[g, piece(stay, quarter)].astype(F32)
        elif step == 1:
            acc[g, piece(at_near, quarter)] += rb[g, half : half + quarter].astype(F32)
            b2, b3 = split_bit(*second), split_bit(*third)
            at = half + quarter
            for n, (p, q) in enumerate(((1 - b2, b3), (b2, 1 - b3), (1 - b2, 1 - b3))):
                away = acc[g, piece(at_near + (2 * p + q) * own, own)]
                sb[g, at + n * own : at + (n + 1) * own] = away.astype(BF16)
            start_all(scatter_copies(g, 2))
        else:
            at = half + quarter
            if step == 2:
                total = acc[g, piece(at_own, own)]
                for n in range(3):
                    total += rb[g, at + n * own : at + (n + 1) * own].astype(F32)
            else:
                here = slice(at + step * own, at + (step + 1) * own)
                total = sb[g, here].astype(F32) + rb[g, here].astype(F32)
            if step < steps - 1:
                sb[g, at + (step + 1) * own : at + (step + 2) * own] = total.astype(BF16)
                start_all(scatter_copies(g, step + 1))
            else:
                full[g, piece(at_own, own)] = total.astype(BF16)
                start_all(gather_copies(g, 0))

    def gather_copies(g, level):
        first, second, third = near_order(g)
        _, at_near, at_own = kept(g)

        def copy(place, slot, flips):
            block = full.at[g, place]
            slot += 2 + steps
            sems = (sum_send.at[g, slot], sum_recv.at[g, slot])
            return remote(block, block, sems, across(*flips))

        if level == 0:
            return [
                copy(piece(at_own, own), n, flips)
                for n, flips in enumerate(([second], [third], [second, third]))
            ]
        if level == 1:
            block = piece(at_near, quarter)
            return [copy(block, 3, [first]), copy(block, 4, [("dp", 1)])]
        other = split_bit("dp", 1) * half + (1 - split_bit(*first)) * quarter
        return [copy(piece(other, quarter), 5, [("dp", 1)])]

    temporal_term(10)
    begin(5)

    fg_sum = dot_nt(later(0), wt_ref[2])
    fg_sum += dot_nt(later(1), wt_ref[1])
    fg_sum += dot_nt(later(2), wt_ref[0])
    fg[...] = fg_sum.astype(BF16).reshape(frames, rows, cols, chan)

    @pl.when(tm == 0)
    def _():
        c0 = c_ref[0].reshape(-1, chan)
        c1 = c_ref[1].reshape(-1, chan)
        fold = dot_nt(c0, wt_ref[0]) + dot_nt(c0, wt_ref[1]) + dot_nt(c1, wt_ref[0])
        fg[0] = (fg_sum[: rows * cols] + fold).astype(BF16).reshape(rows, cols, chan)

    pl.when(has_up)(fg_up.start)
    pl.when(has_down)(fg_down.start)

    temporal_term(9)
    spatial_term(8)
    begin(4)
    for g in range(4):
        spatial_term(2 * g)
        spatial_term(2 * g + 1)
        begin(g)

    store_dec = pltpu.make_async_copy(dec_ref, dec_hbm, store_sem.at[0])
    store_ig = pltpu.make_async_copy(ig_ref, ig_hbm, store_sem.at[1])

    def store_tap(tap):
        g, t = tap // per_group, tap % per_group
        to = sg_hbm.at[tap] if tap < 9 else tg_hbm.at[tap - 9]
        return pltpu.make_async_copy(
            full.at[g, t * chan : (t + 1) * chan], to, store_sem.at[2 + tap]
        )

    def make_decoded(start, count):
        def earlier(back):
            begin_at = start - back
            parts = []
            if begin_at < 0:
                parts.append(soh[2 + begin_at :])
            if begin_at + count > 0:
                parts.append(so[max(begin_at, 0) : begin_at + count])
            value = parts[0] if len(parts) == 1 else jnp.concatenate(parts, axis=0)
            return value.reshape(-1, chan)

        total = dot_nn(earlier(0), wt_ref[2])
        total += dot_nn(earlier(1), wt_ref[1])
        total += dot_nn(earlier(2), wt_ref[0])
        total += x_ref[start : start + count].astype(F32).reshape(-1, chan)
        dec_ref[start : start + count] = total.astype(BF16).reshape(count, rows, cols, chan)

    def decoded_later():
        make_decoded(2, frames - 2)

    def decoded_earlier():
        @pl.when(has_prev)
        def _():
            so_next.wait_recv()

        @pl.when(jnp.logical_not(has_prev))
        def _():
            soh[0] = so[0]
            soh[1] = so[0]

        make_decoded(0, 2)
        store_dec.start()

    def grad_taps_inner():
        taps(t_buf, 1, fg[...].astype(F32), rows, True)

    def grad_taps_outer():
        @pl.when(has_up)
        def _():
            fg_down.wait_recv()

        @pl.when(jnp.logical_not(has_up))
        def _():
            fgh[0] = jnp.zeros((frames, cols, chan), BF16)

        @pl.when(has_down)
        def _():
            fg_up.wait_recv()

        @pl.when(jnp.logical_not(has_down))
        def _():
            fgh[1] = jnp.zeros((frames, cols, chan), BF16)

        taps(t_buf, 0, fgh[0].astype(F32), 1, True)
        taps(t_buf, rows + 1, fgh[1].astype(F32), 1, True)

    def make_input_grad(start, count):
        total = None
        span = slice(start, start + count)
        for i in range(3):
            for j in range(3):
                left = t_buf[span, 2 - i : 2 - i + rows, :, j * chan : (j + 1) * chan]
                term = dot_nt(left.reshape(-1, chan), ws_ref[i, j * chan : (j + 1) * chan])
                total = term if total is None else total + term
        x = x_ref[span].astype(F32).reshape(-1, chan)
        s = sigmoid(x)
        grad = c_ref[span].astype(F32).reshape(-1, chan) + s * (1.0 + x * (1.0 - s)) * total
        ig_ref[span] = grad.astype(BF16).reshape(count, rows, cols, chan)

    def input_grad_first():
        make_input_grad(0, frames // 2)

    def input_grad_second():
        make_input_grad(frames // 2, frames - frames // 2)
        store_ig.start()

    units = [
        decoded_later, grad_taps_inner, decoded_earlier, grad_taps_outer,
        input_grad_first, input_grad_second,
    ]
    order = (5, 4, 0, 1, 2, 3)
    for step in range(steps):
        for n, g in enumerate(order):
            advance(g, step)
            if n in (2, 5) and units:
                units.pop(0)()
    for level in range(3):
        for g in order:
            copies = gather_copies(g, level)
            if level < 2:
                for copy in copies if level == 0 else copies[:1]:
                    copy.wait_recv()
                start_all(gather_copies(g, level + 1))
                continue
            gather_copies(g, 1)[1].wait_recv()
            copies[0].wait_recv()
            for t in range(per_group):
                store_tap(per_group * g + t).start()

    pl.when(has_prev)(c_prev.wait_send)
    pl.when(has_next)(so_next.wait_send)
    for up, down in ((x_up, x_down), (fg_up, fg_down)):
        pl.when(has_up)(up.wait_send)
        pl.when(has_down)(down.wait_send)
    for g in range(GROUPS):
        for step in range(steps):
            for copy in scatter_copies(g, step):
                copy.wait_send()
        for level in range(3):
            for copy in gather_copies(g, level):
                copy.wait_send()
    store_dec.wait()
    store_ig.wait()
    for tap in range(12):
        store_tap(tap).wait()


def write_out(*refs):
    ins, outs, held, sem = refs[:4], refs[4:8], refs[8:12], refs[12]
    parts = [(n, pl.ds(i, 3)) for n in (2, 3) for i in range(0, ins[n].shape[0], 3)]
    parts += [(n, pl.ds(0, ins[n].shape[0])) for n in (0, 1)]

    def copies(source, target, row):
        return [
            pltpu.make_async_copy(source[n].at[at], target[n].at[at], sem.at[row, k])
            for k, (n, at) in enumerate(parts)
        ]

    loads, stores = copies(ins, held, 0), copies(held, outs, 1)
    for load in loads:
        load.start()
    for load, store in zip(loads, stores):
        load.wait()
        store.start()
    for store in stores:
        store.wait()


def local(sizes, frames_in, cotangent, w_spatial, w_temporal):
    x, c = frames_in[0], cotangent[0]
    frames, rows, cols, chan = x.shape
    cell_count = frames * rows * cols * sizes["tm"] * sizes["height"] * sizes["dp"]
    group_rows = 12 * chan // GROUPS
    far = len(far_bits(sizes))
    buffer_rows = group_rows * 3 // 4 + (3 + far) * (group_rows // 16)
    exchanges = 5 + far + 6
    block = jax.ShapeDtypeStruct(x.shape, BF16)
    hbm = pl.BlockSpec(memory_space=pltpu.HBM)
    results = pl.pallas_call(
        functools.partial(kernel, sizes, 1.0 / math.sqrt(cell_count)),
        out_shape=(
            block,
            block,
            jax.ShapeDtypeStruct((9, chan, chan), BF16),
            jax.ShapeDtypeStruct((3, chan, chan), BF16),
        ),
        in_specs=[hbm] * 4,
        out_specs=(hbm,) * 4,
        scratch_shapes=[
            pltpu.VMEM(x.shape, BF16),
            pltpu.VMEM(x.shape, BF16),
            pltpu.VMEM(x.shape, BF16),
            pltpu.VMEM(x.shape, BF16),
            pltpu.VMEM((3, 3 * chan, chan), BF16),
            pltpu.VMEM(w_temporal.shape, BF16),
            pltpu.VMEM((2, frames, cols, chan), BF16),
            pltpu.VMEM((2, rows, cols, chan), BF16),
            pltpu.VMEM((2, rows, cols, chan), BF16),
            pltpu.VMEM((2, frames, cols, chan), BF16),
            pltpu.VMEM(x.shape, BF16),
            pltpu.VMEM(x.shape, BF16),
            pltpu.VMEM((frames, rows + 2, cols, 3 * chan), BF16),
            pltpu.VMEM((frames, rows + 2, cols, 3 * chan), BF16),
            pltpu.VMEM((GROUPS, group_rows, chan), F32),
            pltpu.VMEM((GROUPS, buffer_rows, chan), BF16),
            pltpu.VMEM((GROUPS, buffer_rows, chan), BF16),
            pltpu.VMEM((GROUPS, group_rows, chan), BF16),
            pltpu.SemaphoreType.DMA((4,)),
            pltpu.SemaphoreType.DMA((14,)),
            pltpu.SemaphoreType.DMA((6,)),
            pltpu.SemaphoreType.DMA((6,)),
            pltpu.SemaphoreType.DMA((GROUPS, exchanges)),
            pltpu.SemaphoreType.DMA((GROUPS, exchanges)),
        ],
        compiler_params=pltpu.CompilerParams(
            collective_id=0, has_side_effects=True, vmem_limit_bytes=VMEM_LIMIT
        ),
    )(x, c, w_spatial.reshape(3, 3 * chan, chan), w_temporal)
    decoded, input_grad, spatial, temporal = pl.pallas_call(
        write_out,
        out_shape=tuple(jax.ShapeDtypeStruct(r.shape, r.dtype) for r in results),
        in_specs=[hbm] * 4,
        out_specs=(hbm,) * 4,
        scratch_shapes=[pltpu.VMEM(r.shape, r.dtype) for r in results]
        + [pltpu.SemaphoreType.DMA((2, 6))],
        compiler_params=pltpu.CompilerParams(vmem_limit_bytes=VMEM_LIMIT),
    )(*results)
    return (
        decoded[None],
        input_grad[None],
        spatial.reshape(3, 3, chan, chan),
        temporal.reshape(3, chan, chan),
    )


def solution(mesh):
    sizes = dict(mesh.shape)
    spec = P("dp", "tm", "height", None, None)
    return jax.shard_map(
        functools.partial(local, sizes),
        mesh=mesh,
        in_specs=(spec, spec, P(), P()),
        out_specs=(spec, spec, P(), P()),
        check_vma=False,
    )
```

```python
import functools
import math

import jax
import jax.numpy as jnp
from jax import lax
from jax.experimental import pallas as pl
from jax.experimental.pallas import tpu as pltpu
from jax.sharding import PartitionSpec as P

F32 = jnp.float32
BF16 = jnp.bfloat16
GROUPS = 6
VMEM_LIMIT = 60 * 1024 * 1024


def split_bit(axis, distance):
    return lax.rem(lax.div(lax.axis_index(axis), distance), 2)


def across(*flips):
    place = {}
    for axis, distance in flips:
        index = place.get(axis, lax.axis_index(axis))
        place[axis] = index + distance - 2 * distance * split_bit(axis, distance)
    return place


NEAR = (("tm", 1), ("height", 1), ("tm", 2))


def far_bits(sizes):
    return [
        (axis, 1 << b)
        for axis in ("tm", "height")
        for b in range(sizes[axis].bit_length() - 1)
        if (axis, 1 << b) not in NEAR
    ]


def near_order(g):
    turn = g % len(NEAR)
    return NEAR[turn:] + NEAR[:turn]


def sigmoid(v):
    return 1.0 / (1.0 + jnp.exp(-v))


def shifted(v, cols):
    cells, ch = v.shape
    col = lax.broadcasted_iota(jnp.int32, (cells // cols, cols, ch), 1).reshape(cells, ch)
    before = jnp.where(col == 0, 0.0, pltpu.roll(v, 1, 0))
    after = jnp.where(col == cols - 1, 0.0, pltpu.roll(v, cells - 1, 0))
    return before, after


def dot_nn(a, b):
    return jnp.dot(a, b, preferred_element_type=F32)


def dot_nt(a, b):
    return lax.dot_general(a, b, (((1,), (1,)), ((), ())), preferred_element_type=F32)


def dot_tn(a, b):
    return lax.dot_general(a, b, (((0,), (0,)), ((), ())), preferred_element_type=F32)


def kernel(
    sizes, scale,
    x_hbm, c_hbm, ws_hbm, wt_hbm,
    dec_hbm, ig_hbm, sg_hbm, tg_hbm,
    dec_ref, ig_ref,    x_ref, c_ref, ws_ref, wt_ref, xh, fgh, so, fg, s_buf, t_buf, acc, sb, rb, full,
    load_sem, store_sem, halo_send, halo_recv, sum_send, sum_recv,
):
    frames, rows, cols, chan = x_ref.shape
    cells = frames * rows * cols
    tm, height = lax.axis_index("tm"), lax.axis_index("height")
    n_tm, n_h = sizes["tm"], sizes["height"]
    far = far_bits(sizes)
    per_group = 12 // GROUPS
    group_rows = per_group * chan
    half, quarter, own = group_rows // 2, group_rows // 4, group_rows // 16

    has_prev, has_next = tm > 0, tm < n_tm - 1
    has_up, has_down = height > 0, height < n_h - 1

    loads = [
        pltpu.make_async_copy(src, dst, load_sem.at[n])
        for n, (src, dst) in enumerate(
            ((x_hbm, x_ref), (ws_hbm, ws_ref), (c_hbm, c_ref.at[pl.ds(0, frames)]), (wt_hbm, wt_ref))
        )
    ]
    for load in loads:
        load.start()

    barrier = pltpu.get_barrier_semaphore()

    def greet(device):
        pl.semaphore_signal(barrier, inc=1, device_id=device, device_id_type=pl.DeviceIdType.MESH)

    pairs = [(NEAR[0], NEAR[1]), (NEAR[1], NEAR[2]), (NEAR[2], NEAR[0])]
    partners = [(bit,) for bit in ((("dp", 1),) + NEAR + tuple(far))] + pairs
    for flips in partners:
        greet(across(*flips))
    pl.when(has_prev)(lambda: greet({"tm": tm - 1}))
    pl.when(has_next)(lambda: greet({"tm": tm + 1}))
    pl.when(has_up)(lambda: greet({"height": height - 1}))
    pl.when(has_down)(lambda: greet({"height": height + 1}))
    expected = len(partners) + sum(
        jnp.where(has, 1, 0) for has in (has_prev, has_next, has_up, has_down)
    )
    pl.semaphore_wait(barrier, expected)

    def remote(src, dst, sems, device):
        return pltpu.make_async_remote_copy(
            src_ref=src, dst_ref=dst, send_sem=sems[0], recv_sem=sems[1],
            device_id=device, device_id_type=pl.DeviceIdType.MESH,
        )

    def halo(at):
        return halo_send.at[at], halo_recv.at[at]

    x_up = remote(x_hbm.at[:, 0], xh.at[1], halo(0), {"height": height - 1})
    x_down = remote(x_hbm.at[:, rows - 1], xh.at[0], halo(1), {"height": height + 1})
    c_prev = remote(c_hbm.at[pl.ds(0, 2)], c_ref.at[pl.ds(frames, 2)], halo(2), {"tm": tm - 1})
    so_next = remote(so.at[pl.ds(frames, 2)], so.at[pl.ds(0, 2)], halo(3), {"tm": tm + 1})
    fg_up = remote(fg.at[:, 0], fgh.at[1], halo(4), {"height": height - 1})
    fg_down = remote(fg.at[:, rows - 1], fgh.at[0], halo(5), {"height": height + 1})

    pl.when(has_prev)(c_prev.start)
    pl.when(has_up)(x_up.start)
    pl.when(has_down)(x_down.start)

    def taps(buf, f, part, value, count, flip):
        value = value.reshape(-1, chan)
        before, after = shifted(value, cols)
        if flip:
            before, after = after, before
        for j, v in enumerate((before, value, after)):
            v = v.astype(BF16).reshape(count, cols, chan)
            buf[f, part : part + count, :, j * chan : (j + 1) * chan] = v

    def each_frame(body, first=0, last=frames):
        lax.fori_loop(first, last, lambda f, unused: body(f), None)

    def activation(v):
        v = v.astype(F32)
        return (v * sigmoid(v)).astype(BF16).astype(F32)

    loads[0].wait()
    each_frame(lambda f: taps(s_buf, f, 1, activation(x_ref[f]), rows, False))
    for load in loads[1:]:
        load.wait()

    @pl.when(has_up)
    def _():
        x_down.wait_recv()

    @pl.when(jnp.logical_not(has_up))
    def _():
        xh[0] = jnp.zeros((frames, cols, chan), BF16)

    @pl.when(has_down)
    def _():
        x_up.wait_recv()

    @pl.when(jnp.logical_not(has_down))
    def _():
        xh[1] = jnp.zeros((frames, cols, chan), BF16)

    def spatial_frame(f):
        taps(s_buf, f, 0, activation(xh[0, f]), 1, False)
        taps(s_buf, f, rows + 1, activation(xh[1, f]), 1, False)
        out = None
        for i in range(3):
            left = s_buf[f, i : i + rows].reshape(rows * cols, 3 * chan)
            term = dot_nn(left, ws_ref[i])
            out = term if out is None else out + term
        so[f + 2] = out.astype(BF16).reshape(rows, cols, chan)

    each_frame(spatial_frame)
    pl.when(has_next)(so_next.start)

    def put_term(tap, term):
        g, t = tap // per_group, tap % per_group
        acc[g, t * chan : (t + 1) * chan] = term * scale
        if tap in (9, 10):

            @pl.when(tm == 0)
            def _():
                so0 = so[2].reshape(-1, chan)
                extra = dot_tn(so0, c_ref[0].reshape(-1, chan))
                if tap == 9:
                    extra += dot_tn(so0, c_ref[1].reshape(-1, chan))
                acc[g, t * chan : (t + 1) * chan] += extra * scale

    def temporal_term(tap):
        put_term(tap, dot_tn(so[2:].reshape(cells, chan), later(2 - (tap - 9))))

    def spatial_term(tap):
        i, j = tap // 3, tap % 3
        left = s_buf[:, i : i + rows, :, j * chan : (j + 1) * chan].reshape(cells, chan)
        put_term(tap, dot_tn(left, fg[...].reshape(cells, chan)))

    def later(offset):
        return c_ref[offset : offset + frames].reshape(cells, chan)

    temporal_term(11)

    @pl.when(has_next)
    def _():
        c_prev.wait_recv()

    @pl.when(jnp.logical_not(has_next))
    def _():
        c_ref[frames:] = jnp.zeros((2, rows, cols, chan), BF16)

    def sum_copy(g, at, size, slot, flips):
        place = (g, pl.ds(at, size))
        sems = (sum_send.at[g, slot], sum_recv.at[g, slot])
        return remote(sb.at[place], rb.at[place], sems, across(*flips))

    def piece(start, size):
        return pl.ds(pl.multiple_of(start, size), size)

    def scatter_copies(g, step):
        first, second, third = near_order(g)
        if step == 0:
            return [sum_copy(g, 0, half, 0, [("dp", 1)])]
        if step == 1:
            return [sum_copy(g, half, quarter, 1, [first])]
        at = half + quarter
        if step == 2:
            return [
                sum_copy(g, at + n * own, own, 2 + n, flips)
                for n, flips in enumerate(([second], [third], [second, third]))
            ]
        return [sum_copy(g, at + step * own, own, 2 + step, [far[step - 3]])]

    steps = 3 + len(far)

    def kept(g):
        first, second, third = near_order(g)
        at_dp = split_bit("dp", 1) * half
        at_near = at_dp + split_bit(*first) * quarter
        return at_dp, at_near, at_near + (2 * split_bit(*second) + split_bit(*third)) * own

    def start_all(copies):
        for copy in copies:
            copy.start()

    def begin(g):
        sb[g, :half] = acc[g, piece((1 - split_bit("dp", 1)) * half, half)].astype(BF16)
        start_all(scatter_copies(g, 0))

    def advance(g, step):
        for copy in scatter_copies(g, step):
            copy.wait_recv()
        first, second, third = near_order(g)
        at_dp, at_near, at_own = kept(g)
        if step == 0:
            bit = split_bit(*first)
            away, stay = (1 - bit) * quarter, bit * quarter
            total = acc[g, piece(at_dp + away, quarter)] + rb[g, piece(away, quarter)].astype(F32)
            sb[g, half : half + quarter] = total.astype(BF16)
            start_all(scatter_copies(g, 1))
            acc[g, piece(at_dp + stay, quarter)] += rb[g, piece(stay, quarter)].astype(F32)
        elif step == 1:
            acc[g, piece(at_near, quarter)] += rb[g, half : half + quarter].astype(F32)
            b2, b3 = split_bit(*second), split_bit(*third)
            at = half + quarter
            for n, (p, q) in enumerate(((1 - b2, b3), (b2, 1 - b3), (1 - b2, 1 - b3))):
                away = acc[g, piece(at_near + (2 * p + q) * own, own)]
                sb[g, at + n * own : at + (n + 1) * own] = away.astype(BF16)
            start_all(scatter_copies(g, 2))
        else:
            at = half + quarter
            if step == 2:
                total = acc[g, piece(at_own, own)]
                for n in range(3):
                    total += rb[g, at + n * own : at + (n + 1) * own].astype(F32)
            else:
                here = slice(at + step * own, at + (step + 1) * own)
                total = sb[g, here].astype(F32) + rb[g, here].astype(F32)
            if step < steps - 1:
                sb[g, at + (step + 1) * own : at + (step + 2) * own] = total.astype(BF16)
                start_all(scatter_copies(g, step + 1))
            else:
                full[g, piece(at_own, own)] = total.astype(BF16)
                start_all(gather_copies(g, 0))

    def gather_copies(g, level):
        first, second, third = near_order(g)
        _, at_near, at_own = kept(g)

        def copy(place, slot, flips):
            block = full.at[g, place]
            slot += 2 + steps
            sems = (sum_send.at[g, slot], sum_recv.at[g, slot])
            return remote(block, block, sems, across(*flips))

        if level == 0:
            return [
                copy(piece(at_own, own), n, flips)
                for n, flips in enumerate(([second], [third], [second, third]))
            ]
        if level == 1:
            block = piece(at_near, quarter)
            return [copy(block, 3, [first]), copy(block, 4, [("dp", 1)])]
        other = split_bit("dp", 1) * half + (1 - split_bit(*first)) * quarter
        return [copy(piece(other, quarter), 5, [("dp", 1)])]

    temporal_term(10)
    begin(5)

    def frame_part(f):
        total = dot_nt(c_ref[f].reshape(-1, chan), wt_ref[2])
        total += dot_nt(c_ref[f + 1].reshape(-1, chan), wt_ref[1])
        return total + dot_nt(c_ref[f + 2].reshape(-1, chan), wt_ref[0])

    def put_frame(f, total):
        fg[f] = total.astype(BF16).reshape(rows, cols, chan)

    each_frame(lambda f: put_frame(f, frame_part(f)))

    @pl.when(tm == 0)
    def _():
        c0 = c_ref[0].reshape(-1, chan)
        c1 = c_ref[1].reshape(-1, chan)
        fold = dot_nt(c0, wt_ref[0]) + dot_nt(c0, wt_ref[1]) + dot_nt(c1, wt_ref[0])
        put_frame(0, frame_part(0) + fold)

    pl.when(has_up)(fg_up.start)
    pl.when(has_down)(fg_down.start)

    temporal_term(9)
    spatial_term(8)
    begin(4)
    for g in range(4):
        spatial_term(2 * g)
        spatial_term(2 * g + 1)
        begin(g)

    store_dec = pltpu.make_async_copy(dec_ref, dec_hbm, store_sem.at[0])
    store_ig = pltpu.make_async_copy(ig_ref, ig_hbm, store_sem.at[1])

    def store_tap(tap):
        g, t = tap // per_group, tap % per_group
        to = sg_hbm.at[tap] if tap < 9 else tg_hbm.at[tap - 9]
        return pltpu.make_async_copy(
            full.at[g, t * chan : (t + 1) * chan], to, store_sem.at[2 + tap]
        )

    def make_decoded(f):
        total = x_ref[f].astype(F32).reshape(-1, chan)
        for k in range(3):
            total += dot_nn(so[f + k].reshape(-1, chan), wt_ref[k])
        dec_ref[f] = total.astype(BF16).reshape(rows, cols, chan)

    def decoded_later():
        each_frame(make_decoded, 2, frames)

    def decoded_earlier():
        @pl.when(has_prev)
        def _():
            so_next.wait_recv()

        @pl.when(jnp.logical_not(has_prev))
        def _():
            so[0] = so[2]
            so[1] = so[2]

        each_frame(make_decoded, 0, 2)
        store_dec.start()

    def grad_taps_inner():
        each_frame(lambda f: taps(t_buf, f, 1, fg[f].astype(F32), rows, True))

    def grad_taps_outer():
        @pl.when(has_up)
        def _():
            fg_down.wait_recv()

        @pl.when(jnp.logical_not(has_up))
        def _():
            fgh[0] = jnp.zeros((frames, cols, chan), BF16)

        @pl.when(has_down)
        def _():
            fg_up.wait_recv()

        @pl.when(jnp.logical_not(has_down))
        def _():
            fgh[1] = jnp.zeros((frames, cols, chan), BF16)

        def outer(f):
            taps(t_buf, f, 0, fgh[0, f].astype(F32), 1, True)
            taps(t_buf, f, rows + 1, fgh[1, f].astype(F32), 1, True)

        each_frame(outer)

    def make_input_grad(f):
        total = None
        for i in range(3):
            for j in range(3):
                left = t_buf[f, 2 - i : 2 - i + rows, :, j * chan : (j + 1) * chan]
                term = dot_nt(left.reshape(-1, chan), ws_ref[i, j * chan : (j + 1) * chan])
                total = term if total is None else total + term
        x = x_ref[f].astype(F32).reshape(-1, chan)
        s = sigmoid(x)
        grad = c_ref[f].astype(F32).reshape(-1, chan) + s * (1.0 + x * (1.0 - s)) * total
        ig_ref[f] = grad.astype(BF16).reshape(rows, cols, chan)

    def input_grad_first():
        each_frame(make_input_grad, 0, frames // 2)

    def input_grad_second():
        each_frame(make_input_grad, frames // 2, frames)
        store_ig.start()

    units = [
        decoded_later, grad_taps_inner, decoded_earlier, grad_taps_outer,
        input_grad_first, input_grad_second,
    ]
    order = (5, 4, 0, 1, 2, 3)
    for step in range(steps):
        for n, g in enumerate(order):
            advance(g, step)
            if n in (2, 5) and units:
                units.pop(0)()
    for level in range(3):
        for g in order:
            copies = gather_copies(g, level)
            if level < 2:
                for copy in copies if level == 0 else copies[:1]:
                    copy.wait_recv()
                start_all(gather_copies(g, level + 1))
                continue
            gather_copies(g, 1)[1].wait_recv()
            copies[0].wait_recv()
            for t in range(per_group):
                store_tap(per_group * g + t).start()

    pl.when(has_prev)(c_prev.wait_send)
    pl.when(has_next)(so_next.wait_send)
    for up, down in ((x_up, x_down), (fg_up, fg_down)):
        pl.when(has_up)(up.wait_send)
        pl.when(has_down)(down.wait_send)
    for g in range(GROUPS):
        for step in range(steps):
            for copy in scatter_copies(g, step):
                copy.wait_send()
        for level in range(3):
            for copy in gather_copies(g, level):
                copy.wait_send()
    store_dec.wait()
    store_ig.wait()
    for tap in range(12):
        store_tap(tap).wait()


def write_out(*refs):
    ins, outs, held, sem = refs[:4], refs[4:8], refs[8:12], refs[12]
    parts = [(n, pl.ds(i, 3)) for n in (2, 3) for i in range(0, ins[n].shape[0], 3)]
    parts += [(n, pl.ds(0, ins[n].shape[0])) for n in (0, 1)]

    def copies(source, target, row):
        return [
            pltpu.make_async_copy(source[n].at[at], target[n].at[at], sem.at[row, k])
            for k, (n, at) in enumerate(parts)
        ]

    loads, stores = copies(ins, held, 0), copies(held, outs, 1)
    for load in loads:
        load.start()
    for load, store in zip(loads, stores):
        load.wait()
        store.start()
    for store in stores:
        store.wait()


def local(sizes, frames_in, cotangent, w_spatial, w_temporal):
    x, c = frames_in[0], cotangent[0]
    frames, rows, cols, chan = x.shape
    cell_count = frames * rows * cols * sizes["tm"] * sizes["height"] * sizes["dp"]
    group_rows = 12 * chan // GROUPS
    far = len(far_bits(sizes))
    buffer_rows = group_rows * 3 // 4 + (3 + far) * (group_rows // 16)
    exchanges = 5 + far + 6
    longer = pltpu.VMEM((frames + 2,) + x.shape[1:], BF16)
    block = jax.ShapeDtypeStruct(x.shape, BF16)
    hbm = pl.BlockSpec(memory_space=pltpu.HBM)
    results = pl.pallas_call(
        functools.partial(kernel, sizes, 1.0 / math.sqrt(cell_count)),
        out_shape=(
            block,
            block,
            jax.ShapeDtypeStruct((9, chan, chan), BF16),
            jax.ShapeDtypeStruct((3, chan, chan), BF16),
        ),
        in_specs=[hbm] * 4,
        out_specs=(hbm,) * 4,
        scratch_shapes=[
            pltpu.VMEM(x.shape, BF16),
            pltpu.VMEM(x.shape, BF16),
            pltpu.VMEM(x.shape, BF16),
            longer,
            pltpu.VMEM((3, 3 * chan, chan), BF16),
            pltpu.VMEM(w_temporal.shape, BF16),
            pltpu.VMEM((2, frames, cols, chan), BF16),
            pltpu.VMEM((2, frames, cols, chan), BF16),
            longer,
            pltpu.VMEM(x.shape, BF16),
            pltpu.VMEM((frames, rows + 2, cols, 3 * chan), BF16),
            pltpu.VMEM((frames, rows + 2, cols, 3 * chan), BF16),
            pltpu.VMEM((GROUPS, group_rows, chan), F32),
            pltpu.VMEM((GROUPS, buffer_rows, chan), BF16),
            pltpu.VMEM((GROUPS, buffer_rows, chan), BF16),
            pltpu.VMEM((GROUPS, group_rows, chan), BF16),
            pltpu.SemaphoreType.DMA((4,)),
            pltpu.SemaphoreType.DMA((14,)),
            pltpu.SemaphoreType.DMA((6,)),
            pltpu.SemaphoreType.DMA((6,)),
            pltpu.SemaphoreType.DMA((GROUPS, exchanges)),
            pltpu.SemaphoreType.DMA((GROUPS, exchanges)),
        ],
        compiler_params=pltpu.CompilerParams(
            collective_id=0, has_side_effects=True, vmem_limit_bytes=VMEM_LIMIT
        ),
    )(x, c, w_spatial.reshape(3, 3 * chan, chan), w_temporal)
    decoded, input_grad, spatial, temporal = pl.pallas_call(
        write_out,
        out_shape=tuple(jax.ShapeDtypeStruct(r.shape, r.dtype) for r in results),
        in_specs=[hbm] * 4,
        out_specs=(hbm,) * 4,
        scratch_shapes=[pltpu.VMEM(r.shape, r.dtype) for r in results]
        + [pltpu.SemaphoreType.DMA((2, 6))],
        compiler_params=pltpu.CompilerParams(vmem_limit_bytes=VMEM_LIMIT),
    )(*results)
    return (
        decoded[None],
        input_grad[None],
        spatial.reshape(3, 3, chan, chan),
        temporal.reshape(3, chan, chan),
    )


def solution(mesh):
    sizes = dict(mesh.shape)
    spec = P("dp", "tm", "height", None, None)
    return jax.shard_map(
        functools.partial(local, sizes),
        mesh=mesh,
        in_specs=(spec, spec, P(), P()),
        out_specs=(spec, spec, P(), P()),
        check_vma=False,
    )
```

```python
import functools
import math

import jax
import jax.numpy as jnp
from jax import lax
from jax.experimental import pallas as pl
from jax.experimental.pallas import tpu as pltpu
from jax.sharding import PartitionSpec as P

F32 = jnp.float32
BF16 = jnp.bfloat16
GROUPS = 6
ORDER = (5, 4, 0, 1, 2, 3)
VMEM_LIMIT = 60 * 1024 * 1024


def split_bit(axis, distance):
    return lax.rem(lax.div(lax.axis_index(axis), distance), 2)


def across(*flips):
    place = {}
    for axis, distance in flips:
        index = place.get(axis, lax.axis_index(axis))
        place[axis] = index + distance - 2 * distance * split_bit(axis, distance)
    return place


NEAR = (("tm", 1), ("height", 1), ("tm", 2))


def far_bits(sizes):
    return [
        (axis, 1 << b)
        for axis in ("tm", "height")
        for b in range(sizes[axis].bit_length() - 1)
        if (axis, 1 << b) not in NEAR
    ]


def near_order(g):
    turn = g % len(NEAR)
    return NEAR[turn:] + NEAR[:turn]


def sigmoid(v):
    return 1.0 / (1.0 + jnp.exp(-v))


def shifted(v, cols):
    cells, ch = v.shape
    col = lax.broadcasted_iota(jnp.int32, (cells // cols, cols, ch), 1).reshape(cells, ch)
    before = jnp.where(col == 0, 0.0, pltpu.roll(v, 1, 0))
    after = jnp.where(col == cols - 1, 0.0, pltpu.roll(v, cells - 1, 0))
    return before, after


def dot_nn(a, b):
    return jnp.dot(a, b, preferred_element_type=F32)


def dot_nt(a, b):
    return lax.dot_general(a, b, (((1,), (1,)), ((), ())), preferred_element_type=F32)


def dot_tn(a, b):
    return lax.dot_general(a, b, (((0,), (0,)), ((), ())), preferred_element_type=F32)


def kernel(
    sizes, scale,
    x_hbm, c_hbm, ws_hbm, wt_hbm,
    dec_hbm, ig_hbm, sg_hbm, tg_hbm,
    dec_ref, ig_ref,    x_ref, c_ref, ws_ref, wt_ref, xh, ch, soh, fgh, so, fg, s_buf, t_buf, acc, sb, rb, full,
    load_sem, store_sem, halo_send, halo_recv, sum_send, sum_recv,
):
    frames, rows, cols, chan = x_ref.shape
    cells = frames * rows * cols
    tm, height = lax.axis_index("tm"), lax.axis_index("height")
    n_tm, n_h = sizes["tm"], sizes["height"]
    far = far_bits(sizes)
    per_group = 12 // GROUPS
    group_rows = per_group * chan
    half, quarter, own = group_rows // 2, group_rows // 4, group_rows // 16

    has_prev, has_next = tm > 0, tm < n_tm - 1
    has_up, has_down = height > 0, height < n_h - 1

    loads = [
        pltpu.make_async_copy(src, dst, load_sem.at[n])
        for n, (src, dst) in enumerate(
            ((x_hbm, x_ref), (ws_hbm, ws_ref), (c_hbm, c_ref), (wt_hbm, wt_ref))
        )
    ]
    for load in loads:
        load.start()

    barrier = pltpu.get_barrier_semaphore()

    def greet(device):
        pl.semaphore_signal(barrier, inc=1, device_id=device, device_id_type=pl.DeviceIdType.MESH)

    pairs = [(NEAR[0], NEAR[1]), (NEAR[1], NEAR[2]), (NEAR[2], NEAR[0])]
    partners = [(bit,) for bit in ((("dp", 1),) + NEAR + tuple(far))] + pairs
    for flips in partners:
        greet(across(*flips))
    pl.when(has_prev)(lambda: greet({"tm": tm - 1}))
    pl.when(has_next)(lambda: greet({"tm": tm + 1}))
    pl.when(has_up)(lambda: greet({"height": height - 1}))
    pl.when(has_down)(lambda: greet({"height": height + 1}))
    expected = len(partners) + sum(
        jnp.where(has, 1, 0) for has in (has_prev, has_next, has_up, has_down)
    )
    pl.semaphore_wait(barrier, expected)

    def remote(src, dst, sems, device):
        return pltpu.make_async_remote_copy(
            src_ref=src, dst_ref=dst, send_sem=sems[0], recv_sem=sems[1],
            device_id=device, device_id_type=pl.DeviceIdType.MESH,
        )

    def halo(at):
        return halo_send.at[at], halo_recv.at[at]

    x_up = remote(x_hbm.at[:, 0], xh.at[1], halo(0), {"height": height - 1})
    x_down = remote(x_hbm.at[:, rows - 1], xh.at[0], halo(1), {"height": height + 1})
    c_prev = remote(c_hbm.at[pl.ds(0, 2)], ch, halo(2), {"tm": tm - 1})
    so_next = remote(so.at[pl.ds(frames - 2, 2)], soh, halo(3), {"tm": tm + 1})
    fg_up = remote(fg.at[:, 0], fgh.at[1], halo(4), {"height": height - 1})
    fg_down = remote(fg.at[:, rows - 1], fgh.at[0], halo(5), {"height": height + 1})

    pl.when(has_prev)(c_prev.start)
    pl.when(has_up)(x_up.start)
    pl.when(has_down)(x_down.start)

    def taps(buf, part, value, count, flip):
        value = value.reshape(-1, chan)
        before, after = shifted(value, cols)
        if flip:
            before, after = after, before
        for j, v in enumerate((before, value, after)):
            v = v.astype(BF16).reshape(frames, count, cols, chan)
            buf[:, part : part + count, :, j * chan : (j + 1) * chan] = v

    def activation(v):
        v = v.astype(F32)
        return (v * sigmoid(v)).astype(BF16).astype(F32)

    loads[0].wait()
    taps(s_buf, 1, activation(x_ref[...]), rows, False)
    for load in loads[1:]:
        load.wait()

    @pl.when(has_up)
    def _():
        x_down.wait_recv()

    @pl.when(jnp.logical_not(has_up))
    def _():
        xh[0] = jnp.zeros((frames, cols, chan), BF16)

    @pl.when(has_down)
    def _():
        x_up.wait_recv()

    @pl.when(jnp.logical_not(has_down))
    def _():
        xh[1] = jnp.zeros((frames, cols, chan), BF16)

    taps(s_buf, 0, activation(xh[0]), 1, False)
    taps(s_buf, rows + 1, activation(xh[1]), 1, False)

    def s_rows(i):
        return s_buf[:, i : i + rows].reshape(cells, 3 * chan)

    out = dot_nn(s_rows(0), ws_ref[0])
    out += dot_nn(s_rows(1), ws_ref[1])
    out += dot_nn(s_rows(2), ws_ref[2])
    so[...] = out.astype(BF16).reshape(frames, rows, cols, chan)

    def put_term(tap, term):
        g, t = tap // per_group, tap % per_group
        acc[g, t * chan : (t + 1) * chan] = term * scale
        if tap in (9, 10):

            @pl.when(tm == 0)
            def _():
                so0 = so[0].reshape(-1, chan)
                extra = dot_tn(so0, c_ref[0].reshape(-1, chan))
                if tap == 9:
                    extra += dot_tn(so0, c_ref[1].reshape(-1, chan))
                acc[g, t * chan : (t + 1) * chan] += extra * scale

    def temporal_term(tap):
        put_term(tap, dot_tn(so[...].reshape(cells, chan), later(2 - (tap - 9))))

    def spatial_term(tap):
        i, j = tap // 3, tap % 3
        left = s_buf[:, i : i + rows, :, j * chan : (j + 1) * chan].reshape(cells, chan)
        put_term(tap, dot_tn(left, fg[...].reshape(cells, chan)))

    def later(offset):
        if offset == 0:
            return c_ref[...].reshape(cells, chan)
        parts = [c_ref[offset:], ch[:offset]]
        return jnp.concatenate(parts, axis=0).reshape(cells, chan)

    temporal_term(11)

    @pl.when(has_next)
    def _():
        c_prev.wait_recv()

    @pl.when(jnp.logical_not(has_next))
    def _():
        ch[...] = jnp.zeros(ch.shape, BF16)

    pl.when(has_next)(so_next.start)

    def sum_copy(g, at, size, slot, flips):
        place = (g, pl.ds(at, size))
        sems = (sum_send.at[g, slot], sum_recv.at[g, slot])
        return remote(sb.at[place], rb.at[place], sems, across(*flips))

    def piece(start, size):
        return pl.ds(pl.multiple_of(start, size), size)

    def scatter_copies(g, step):
        first, second, third = near_order(g)
        if step == 0:
            return [sum_copy(g, 0, half, 0, [("dp", 1)])]
        if step == 1:
            return [sum_copy(g, half, quarter, 1, [first])]
        at = half + quarter
        if step == 2:
            return [
                sum_copy(g, at + n * own, own, 2 + n, flips)
                for n, flips in enumerate(([second], [third], [second, third]))
            ]
        return [sum_copy(g, at + step * own, own, 2 + step, [far[step - 3]])]

    steps = 3 + len(far)

    def kept(g):
        first, second, third = near_order(g)
        at_dp = split_bit("dp", 1) * half
        at_near = at_dp + split_bit(*first) * quarter
        return at_dp, at_near, at_near + (2 * split_bit(*second) + split_bit(*third)) * own

    def start_all(copies):
        for copy in copies:
            copy.start()

    def begin(g):
        sb[g, :half] = acc[g, piece((1 - split_bit("dp", 1)) * half, half)].astype(BF16)
        start_all(scatter_copies(g, 0))

    def advance(g, step):
        for copy in scatter_copies(g, step):
            copy.wait_recv()
        first, second, third = near_order(g)
        at_dp, at_near, at_own = kept(g)
        if step == 0:
            bit = split_bit(*first)
            away, stay = (1 - bit) * quarter, bit * quarter
            total = acc[g, piece(at_dp + away, quarter)] + rb[g, piece(away, quarter)].astype(F32)
            sb[g, half : half + quarter] = total.astype(BF16)
            start_all(scatter_copies(g, 1))
            acc[g, piece(at_dp + stay, quarter)] += rb[g, piece(stay, quarter)].astype(F32)
        elif step == 1:
            acc[g, piece(at_near, quarter)] += rb[g, half : half + quarter].astype(F32)
            b2, b3 = split_bit(*second), split_bit(*third)
            at = half + quarter
            for n, (p, q) in enumerate(((1 - b2, b3), (b2, 1 - b3), (1 - b2, 1 - b3))):
                away = acc[g, piece(at_near + (2 * p + q) * own, own)]
                sb[g, at + n * own : at + (n + 1) * own] = away.astype(BF16)
            start_all(scatter_copies(g, 2))
        else:
            at = half + quarter
            if step == 2:
                total = acc[g, piece(at_own, own)]
                for n in range(3):
                    total += rb[g, at + n * own : at + (n + 1) * own].astype(F32)
            else:
                here = slice(at + step * own, at + (step + 1) * own)
                total = sb[g, here].astype(F32) + rb[g, here].astype(F32)
            if step < steps - 1:
                sb[g, at + (step + 1) * own : at + (step + 2) * own] = total.astype(BF16)
                start_all(scatter_copies(g, step + 1))
            else:
                full[g, piece(at_own, own)] = total.astype(BF16)
                start_all(gather_copies(g, 0))

    def gather_copies(g, level):
        first, second, third = near_order(g)
        _, at_near, at_own = kept(g)

        def copy(place, slot, flips):
            block = full.at[g, place]
            slot += 2 + steps
            sems = (sum_send.at[g, slot], sum_recv.at[g, slot])
            return remote(block, block, sems, across(*flips))

        if level == 0:
            return [
                copy(piece(at_own, own), n, flips)
                for n, flips in enumerate(([second], [third], [second, third]))
            ]
        if level == 1:
            block = piece(at_near, quarter)
            return [copy(block, 3, [first]), copy(block, 4, [("dp", 1)])]
        other = split_bit("dp", 1) * half + (1 - split_bit(*first)) * quarter
        return [copy(piece(other, quarter), 5, [("dp", 1)])]

    temporal_term(10)
    begin(ORDER[0])

    fg_sum = dot_nt(later(0), wt_ref[2])
    fg_sum += dot_nt(later(1), wt_ref[1])
    fg_sum += dot_nt(later(2), wt_ref[0])
    fg[...] = fg_sum.astype(BF16).reshape(frames, rows, cols, chan)

    @pl.when(tm == 0)
    def _():
        c0 = c_ref[0].reshape(-1, chan)
        c1 = c_ref[1].reshape(-1, chan)
        fold = dot_nt(c0, wt_ref[0]) + dot_nt(c0, wt_ref[1]) + dot_nt(c1, wt_ref[0])
        fg[0] = (fg_sum[: rows * cols] + fold).astype(BF16).reshape(rows, cols, chan)

    pl.when(has_up)(fg_up.start)
    pl.when(has_down)(fg_down.start)

    store_dec = pltpu.make_async_copy(dec_ref, dec_hbm, store_sem.at[0])
    store_ig = pltpu.make_async_copy(ig_ref, ig_hbm, store_sem.at[1])

    def store_tap(tap):
        g, t = tap // per_group, tap % per_group
        to = sg_hbm.at[tap] if tap < 9 else tg_hbm.at[tap - 9]
        return pltpu.make_async_copy(
            full.at[g, t * chan : (t + 1) * chan], to, store_sem.at[2 + tap]
        )

    def make_decoded(start, count):
        def earlier(back):
            begin_at = start - back
            parts = []
            if begin_at < 0:
                parts.append(soh[2 + begin_at :])
            if begin_at + count > 0:
                parts.append(so[max(begin_at, 0) : begin_at + count])
            value = parts[0] if len(parts) == 1 else jnp.concatenate(parts, axis=0)
            return value.reshape(-1, chan)

        total = dot_nn(earlier(0), wt_ref[2])
        total += dot_nn(earlier(1), wt_ref[1])
        total += dot_nn(earlier(2), wt_ref[0])
        total += x_ref[start : start + count].astype(F32).reshape(-1, chan)
        dec_ref[start : start + count] = total.astype(BF16).reshape(count, rows, cols, chan)

    def decoded_later():
        make_decoded(2, frames - 2)

    def decoded_earlier():
        @pl.when(has_prev)
        def _():
            so_next.wait_recv()

        @pl.when(jnp.logical_not(has_prev))
        def _():
            soh[0] = so[0]
            soh[1] = so[0]

        make_decoded(0, 2)
        store_dec.start()

    def grad_taps_inner():
        taps(t_buf, 1, fg[...].astype(F32), rows, True)

    def grad_taps_outer():
        @pl.when(has_up)
        def _():
            fg_down.wait_recv()

        @pl.when(jnp.logical_not(has_up))
        def _():
            fgh[0] = jnp.zeros((frames, cols, chan), BF16)

        @pl.when(has_down)
        def _():
            fg_up.wait_recv()

        @pl.when(jnp.logical_not(has_down))
        def _():
            fgh[1] = jnp.zeros((frames, cols, chan), BF16)

        taps(t_buf, 0, fgh[0].astype(F32), 1, True)
        taps(t_buf, rows + 1, fgh[1].astype(F32), 1, True)

    def make_input_grad(start, count):
        total = None
        span = slice(start, start + count)
        for i in range(3):
            for j in range(3):
                left = t_buf[span, 2 - i : 2 - i + rows, :, j * chan : (j + 1) * chan]
                term = dot_nt(left.reshape(-1, chan), ws_ref[i, j * chan : (j + 1) * chan])
                total = term if total is None else total + term
        x = x_ref[span].astype(F32).reshape(-1, chan)
        s = sigmoid(x)
        grad = c_ref[span].astype(F32).reshape(-1, chan) + s * (1.0 + x * (1.0 - s)) * total
        ig_ref[span] = grad.astype(BF16).reshape(count, rows, cols, chan)

    def gather(g, level):
        copies = gather_copies(g, level)
        if level < 2:
            for copy in copies if level == 0 else copies[:1]:
                copy.wait_recv()
            start_all(gather_copies(g, level + 1))
            return
        gather_copies(g, 1)[1].wait_recv()
        copies[0].wait_recv()
        for t in range(per_group):
            store_tap(per_group * g + t).start()

    def terms(g):
        for tap in range(per_group * g, per_group * g + per_group):
            temporal_term(tap) if tap >= 9 else spatial_term(tap)
        begin(g)

    events = []
    for n, g in enumerate(ORDER):
        if n > 0:
            events.append((n, functools.partial(terms, g)))
        for step in range(steps):
            after = (2, 5, 8)[step] if step < 3 else 8 + 4 * (step - 2)
            events.append((n + after + 0.1, functools.partial(advance, g, step)))
        for level in range(3):
            after = 8 + 4 * (steps - 3) + 3 * (level + 1)
            events.append((n + after + 0.2, functools.partial(gather, g, level)))
    units = [decoded_later, grad_taps_inner, decoded_earlier, grad_taps_outer]
    units += [functools.partial(make_input_grad, f, 1) for f in range(frames)] + [store_ig.start]
    for n, unit in enumerate(units):
        events.append((GROUPS + 0.5 + n, unit))
    for _, event in sorted(events, key=lambda e: e[0]):
        event()

    pl.when(has_prev)(c_prev.wait_send)
    pl.when(has_next)(so_next.wait_send)
    for up, down in ((x_up, x_down), (fg_up, fg_down)):
        pl.when(has_up)(up.wait_send)
        pl.when(has_down)(down.wait_send)
    for g in range(GROUPS):
        for step in range(steps):
            for copy in scatter_copies(g, step):
                copy.wait_send()
        for level in range(3):
            for copy in gather_copies(g, level):
                copy.wait_send()
    store_dec.wait()
    store_ig.wait()
    for tap in range(12):
        store_tap(tap).wait()


def write_out(*refs):
    ins, outs, held, sem = refs[:4], refs[4:8], refs[8:12], refs[12]
    parts = [(n, pl.ds(i, 3)) for n in (2, 3) for i in range(0, ins[n].shape[0], 3)]
    parts += [(n, pl.ds(0, ins[n].shape[0])) for n in (0, 1)]

    def copies(source, target, row):
        return [
            pltpu.make_async_copy(source[n].at[at], target[n].at[at], sem.at[row, k])
            for k, (n, at) in enumerate(parts)
        ]

    loads, stores = copies(ins, held, 0), copies(held, outs, 1)
    for load in loads:
        load.start()
    for load, store in zip(loads, stores):
        load.wait()
        store.start()
    for store in stores:
        store.wait()


def local(sizes, frames_in, cotangent, w_spatial, w_temporal):
    x, c = frames_in[0], cotangent[0]
    frames, rows, cols, chan = x.shape
    cell_count = frames * rows * cols * sizes["tm"] * sizes["height"] * sizes["dp"]
    group_rows = 12 * chan // GROUPS
    far = len(far_bits(sizes))
    buffer_rows = group_rows * 3 // 4 + (3 + far) * (group_rows // 16)
    exchanges = 5 + far + 6
    block = jax.ShapeDtypeStruct(x.shape, BF16)
    hbm = pl.BlockSpec(memory_space=pltpu.HBM)
    results = pl.pallas_call(
        functools.partial(kernel, sizes, 1.0 / math.sqrt(cell_count)),
        out_shape=(
            block,
            block,
            jax.ShapeDtypeStruct((9, chan, chan), BF16),
            jax.ShapeDtypeStruct((3, chan, chan), BF16),
        ),
        in_specs=[hbm] * 4,
        out_specs=(hbm,) * 4,
        scratch_shapes=[
            pltpu.VMEM(x.shape, BF16),
            pltpu.VMEM(x.shape, BF16),
            pltpu.VMEM(x.shape, BF16),
            pltpu.VMEM(x.shape, BF16),
            pltpu.VMEM((3, 3 * chan, chan), BF16),
            pltpu.VMEM(w_temporal.shape, BF16),
            pltpu.VMEM((2, frames, cols, chan), BF16),
            pltpu.VMEM((2, rows, cols, chan), BF16),
            pltpu.VMEM((2, rows, cols, chan), BF16),
            pltpu.VMEM((2, frames, cols, chan), BF16),
            pltpu.VMEM(x.shape, BF16),
            pltpu.VMEM(x.shape, BF16),
            pltpu.VMEM((frames, rows + 2, cols, 3 * chan), BF16),
            pltpu.VMEM((frames, rows + 2, cols, 3 * chan), BF16),
            pltpu.VMEM((GROUPS, group_rows, chan), F32),
            pltpu.VMEM((GROUPS, buffer_rows, chan), BF16),
            pltpu.VMEM((GROUPS, buffer_rows, chan), BF16),
            pltpu.VMEM((GROUPS, group_rows, chan), BF16),
            pltpu.SemaphoreType.DMA((4,)),
            pltpu.SemaphoreType.DMA((14,)),
            pltpu.SemaphoreType.DMA((6,)),
            pltpu.SemaphoreType.DMA((6,)),
            pltpu.SemaphoreType.DMA((GROUPS, exchanges)),
            pltpu.SemaphoreType.DMA((GROUPS, exchanges)),
        ],
        compiler_params=pltpu.CompilerParams(
            collective_id=0, has_side_effects=True, vmem_limit_bytes=VMEM_LIMIT
        ),
    )(x, c, w_spatial.reshape(3, 3 * chan, chan), w_temporal)
    decoded, input_grad, spatial, temporal = pl.pallas_call(
        write_out,
        out_shape=tuple(jax.ShapeDtypeStruct(r.shape, r.dtype) for r in results),
        in_specs=[hbm] * 4,
        out_specs=(hbm,) * 4,
        scratch_shapes=[pltpu.VMEM(r.shape, r.dtype) for r in results]
        + [pltpu.SemaphoreType.DMA((2, 6))],
        compiler_params=pltpu.CompilerParams(vmem_limit_bytes=VMEM_LIMIT),
    )(*results)
    return (
        decoded[None],
        input_grad[None],
        spatial.reshape(3, 3, chan, chan),
        temporal.reshape(3, chan, chan),
    )


def solution(mesh):
    sizes = dict(mesh.shape)
    spec = P("dp", "tm", "height", None, None)
    return jax.shard_map(
        functools.partial(local, sizes),
        mesh=mesh,
        in_specs=(spec, spec, P(), P()),
        out_specs=(spec, spec, P(), P()),
        check_vma=False,
    )
```

```python
import functools
import math

import jax
import jax.numpy as jnp
from jax import lax
from jax.experimental import pallas as pl
from jax.experimental.pallas import tpu as pltpu
from jax.sharding import PartitionSpec as P

F32 = jnp.float32
BF16 = jnp.bfloat16
GROUPS = 6
ORDER = (5, 4, 0, 1, 2, 3)
VMEM_LIMIT = 60 * 1024 * 1024


def split_bit(axis, distance):
    return lax.rem(lax.div(lax.axis_index(axis), distance), 2)


def across(*flips):
    place = {}
    for axis, distance in flips:
        index = place.get(axis, lax.axis_index(axis))
        place[axis] = index + distance - 2 * distance * split_bit(axis, distance)
    return place


NEAR = (("tm", 1), ("height", 1), ("tm", 2))


def far_bits(sizes):
    return [
        (axis, 1 << b)
        for axis in ("tm", "height")
        for b in range(sizes[axis].bit_length() - 1)
        if (axis, 1 << b) not in NEAR
    ]


def near_order(g):
    turn = g % len(NEAR)
    return NEAR[turn:] + NEAR[:turn]


def sigmoid(v):
    return 1.0 / (1.0 + jnp.exp(-v))


def shifted(v, cols):
    cells, ch = v.shape
    col = lax.broadcasted_iota(jnp.int32, (cells // cols, cols, ch), 1).reshape(cells, ch)
    before = jnp.where(col == 0, 0.0, pltpu.roll(v, 1, 0))
    after = jnp.where(col == cols - 1, 0.0, pltpu.roll(v, cells - 1, 0))
    return before, after


def dot_nn(a, b):
    return jnp.dot(a, b, preferred_element_type=F32)


def dot_nt(a, b):
    return lax.dot_general(a, b, (((1,), (1,)), ((), ())), preferred_element_type=F32)


def dot_tn(a, b):
    return lax.dot_general(a, b, (((0,), (0,)), ((), ())), preferred_element_type=F32)


def kernel(
    sizes, scale,
    x_hbm, c_hbm, ws_hbm, wt_hbm,
    dec_hbm, ig_hbm, sg_hbm, tg_hbm,
    dec_ref, ig_ref,    x_ref, c_ref, ws_ref, wt_ref, xh, ch, soh, fgh, so, fg, s_buf, t_buf, acc, sb, rb, full, turned, so_t, fg_t,
    load_sem, store_sem, halo_send, halo_recv, sum_send, sum_recv,
):
    frames, rows, cols, chan = x_ref.shape
    cells = frames * rows * cols
    tm, height = lax.axis_index("tm"), lax.axis_index("height")
    n_tm, n_h = sizes["tm"], sizes["height"]
    far = far_bits(sizes)
    per_group = 12 // GROUPS
    group_rows = per_group * chan
    half, quarter, own = group_rows // 2, group_rows // 4, group_rows // 16

    has_prev, has_next = tm > 0, tm < n_tm - 1
    has_up, has_down = height > 0, height < n_h - 1

    loads = [
        pltpu.make_async_copy(src, dst, load_sem.at[n])
        for n, (src, dst) in enumerate(
            ((x_hbm, x_ref), (ws_hbm, ws_ref), (c_hbm, c_ref), (wt_hbm, wt_ref))
        )
    ]
    for load in loads:
        load.start()

    barrier = pltpu.get_barrier_semaphore()

    def greet(device):
        pl.semaphore_signal(barrier, inc=1, device_id=device, device_id_type=pl.DeviceIdType.MESH)

    pairs = [(NEAR[0], NEAR[1]), (NEAR[1], NEAR[2]), (NEAR[2], NEAR[0])]
    partners = [(bit,) for bit in ((("dp", 1),) + NEAR + tuple(far))] + pairs
    for flips in partners:
        greet(across(*flips))
    pl.when(has_prev)(lambda: greet({"tm": tm - 1}))
    pl.when(has_next)(lambda: greet({"tm": tm + 1}))
    pl.when(has_up)(lambda: greet({"height": height - 1}))
    pl.when(has_down)(lambda: greet({"height": height + 1}))
    expected = len(partners) + sum(
        jnp.where(has, 1, 0) for has in (has_prev, has_next, has_up, has_down)
    )
    pl.semaphore_wait(barrier, expected)

    def remote(src, dst, sems, device):
        return pltpu.make_async_remote_copy(
            src_ref=src, dst_ref=dst, send_sem=sems[0], recv_sem=sems[1],
            device_id=device, device_id_type=pl.DeviceIdType.MESH,
        )

    def halo(at):
        return halo_send.at[at], halo_recv.at[at]

    x_up = remote(x_hbm.at[:, 0], xh.at[1], halo(0), {"height": height - 1})
    x_down = remote(x_hbm.at[:, rows - 1], xh.at[0], halo(1), {"height": height + 1})
    c_prev = remote(c_hbm.at[pl.ds(0, 2)], ch, halo(2), {"tm": tm - 1})
    so_next = remote(so.at[pl.ds(frames - 2, 2)], soh, halo(3), {"tm": tm + 1})
    fg_up = remote(fg.at[:, 0], fgh.at[1], halo(4), {"height": height - 1})
    fg_down = remote(fg.at[:, rows - 1], fgh.at[0], halo(5), {"height": height + 1})

    pl.when(has_prev)(c_prev.start)
    pl.when(has_up)(x_up.start)
    pl.when(has_down)(x_down.start)

    def taps(buf, part, value, count, flip):
        value = value.reshape(-1, chan)
        before, after = shifted(value, cols)
        if flip:
            before, after = after, before
        for j, v in enumerate((before, value, after)):
            v = v.astype(BF16).reshape(frames, count, cols, chan)
            buf[:, part : part + count, :, j * chan : (j + 1) * chan] = v

    def activation(v):
        v = v.astype(F32)
        return (v * sigmoid(v)).astype(BF16).astype(F32)

    loads[0].wait()
    taps(s_buf, 1, activation(x_ref[...]), rows, False)
    for load in loads[1:]:
        load.wait()

    @pl.when(has_up)
    def _():
        x_down.wait_recv()

    @pl.when(jnp.logical_not(has_up))
    def _():
        xh[0] = jnp.zeros((frames, cols, chan), BF16)

    @pl.when(has_down)
    def _():
        x_up.wait_recv()

    @pl.when(jnp.logical_not(has_down))
    def _():
        xh[1] = jnp.zeros((frames, cols, chan), BF16)

    taps(s_buf, 0, activation(xh[0]), 1, False)
    taps(s_buf, rows + 1, activation(xh[1]), 1, False)

    def s_rows(i):
        return s_buf[:, i : i + rows].reshape(cells, 3 * chan)

    out = dot_nn(s_rows(0), ws_ref[0])
    out += dot_nn(s_rows(1), ws_ref[1])
    out += dot_nn(s_rows(2), ws_ref[2])
    so[...] = out.astype(BF16).reshape(frames, rows, cols, chan)

    def put_term(tap, term):
        g, t = tap // per_group, tap % per_group
        acc[g, t * chan : (t + 1) * chan] = term * scale
        if tap in (9, 10):

            @pl.when(tm == 0)
            def _():
                so0 = so[0].reshape(-1, chan)
                extra = dot_tn(so0, c_ref[0].reshape(-1, chan))
                if tap == 9:
                    extra += dot_tn(so0, c_ref[1].reshape(-1, chan))
                acc[g, t * chan : (t + 1) * chan] += extra * scale

    def temporal_term(tap):
        put_term(tap, dot_nn(so_t[...], later(2 - (tap - 9))))

    def spatial_term(tap):
        i, j = tap // 3, tap % 3
        left = s_buf[:, i : i + rows, :, j * chan : (j + 1) * chan].reshape(cells, chan)
        put_term(tap, dot_nn(fg_t[...], left))

    def later(offset):
        if offset == 0:
            return c_ref[...].reshape(cells, chan)
        parts = [c_ref[offset:], ch[:offset]]
        return jnp.concatenate(parts, axis=0).reshape(cells, chan)

    so_t[...] = so[...].reshape(cells, chan).T
    temporal_term(11)

    @pl.when(has_next)
    def _():
        c_prev.wait_recv()

    @pl.when(jnp.logical_not(has_next))
    def _():
        ch[...] = jnp.zeros(ch.shape, BF16)

    pl.when(has_next)(so_next.start)

    def sum_copy(g, at, size, slot, flips):
        place = (g, pl.ds(at, size))
        sems = (sum_send.at[g, slot], sum_recv.at[g, slot])
        return remote(sb.at[place], rb.at[place], sems, across(*flips))

    def piece(start, size):
        return pl.ds(pl.multiple_of(start, size), size)

    def scatter_copies(g, step):
        first, second, third = near_order(g)
        if step == 0:
            return [sum_copy(g, 0, half, 0, [("dp", 1)])]
        if step == 1:
            return [sum_copy(g, half, quarter, 1, [first])]
        at = half + quarter
        if step == 2:
            return [
                sum_copy(g, at + n * own, own, 2 + n, flips)
                for n, flips in enumerate(([second], [third], [second, third]))
            ]
        return [sum_copy(g, at + step * own, own, 2 + step, [far[step - 3]])]

    steps = 3 + len(far)

    def kept(g):
        first, second, third = near_order(g)
        at_dp = split_bit("dp", 1) * half
        at_near = at_dp + split_bit(*first) * quarter
        return at_dp, at_near, at_near + (2 * split_bit(*second) + split_bit(*third)) * own

    def start_all(copies):
        for copy in copies:
            copy.start()

    def begin(g):
        sb[g, :half] = acc[g, piece((1 - split_bit("dp", 1)) * half, half)].astype(BF16)
        start_all(scatter_copies(g, 0))

    def advance(g, step):
        for copy in scatter_copies(g, step):
            copy.wait_recv()
        first, second, third = near_order(g)
        at_dp, at_near, at_own = kept(g)
        if step == 0:
            bit = split_bit(*first)
            away, stay = (1 - bit) * quarter, bit * quarter
            total = acc[g, piece(at_dp + away, quarter)] + rb[g, piece(away, quarter)].astype(F32)
            sb[g, half : half + quarter] = total.astype(BF16)
            start_all(scatter_copies(g, 1))
            acc[g, piece(at_dp + stay, quarter)] += rb[g, piece(stay, quarter)].astype(F32)
        elif step == 1:
            acc[g, piece(at_near, quarter)] += rb[g, half : half + quarter].astype(F32)
            b2, b3 = split_bit(*second), split_bit(*third)
            at = half + quarter
            for n, (p, q) in enumerate(((1 - b2, b3), (b2, 1 - b3), (1 - b2, 1 - b3))):
                away = acc[g, piece(at_near + (2 * p + q) * own, own)]
                sb[g, at + n * own : at + (n + 1) * own] = away.astype(BF16)
            start_all(scatter_copies(g, 2))
        else:
            at = half + quarter
            if step == 2:
                total = acc[g, piece(at_own, own)]
                for n in range(3):
                    total += rb[g, at + n * own : at + (n + 1) * own].astype(F32)
            else:
                here = slice(at + step * own, at + (step + 1) * own)
                total = sb[g, here].astype(F32) + rb[g, here].astype(F32)
            if step < steps - 1:
                sb[g, at + (step + 1) * own : at + (step + 2) * own] = total.astype(BF16)
                start_all(scatter_copies(g, step + 1))
            else:
                full[g, piece(at_own, own)] = total.astype(BF16)
                start_all(gather_copies(g, 0))

    def gather_copies(g, level):
        first, second, third = near_order(g)
        _, at_near, at_own = kept(g)

        def copy(place, slot, flips):
            block = full.at[g, place]
            slot += 2 + steps
            sems = (sum_send.at[g, slot], sum_recv.at[g, slot])
            return remote(block, block, sems, across(*flips))

        if level == 0:
            return [
                copy(piece(at_own, own), n, flips)
                for n, flips in enumerate(([second], [third], [second, third]))
            ]
        if level == 1:
            block = piece(at_near, quarter)
            return [copy(block, 3, [first]), copy(block, 4, [("dp", 1)])]
        other = split_bit("dp", 1) * half + (1 - split_bit(*first)) * quarter
        return [copy(piece(other, quarter), 5, [("dp", 1)])]

    temporal_term(10)
    begin(ORDER[0])

    fg_sum = dot_nt(later(0), wt_ref[2])
    fg_sum += dot_nt(later(1), wt_ref[1])
    fg_sum += dot_nt(later(2), wt_ref[0])
    fg[...] = fg_sum.astype(BF16).reshape(frames, rows, cols, chan)

    @pl.when(tm == 0)
    def _():
        c0 = c_ref[0].reshape(-1, chan)
        c1 = c_ref[1].reshape(-1, chan)
        fold = dot_nt(c0, wt_ref[0]) + dot_nt(c0, wt_ref[1]) + dot_nt(c1, wt_ref[0])
        fg[0] = (fg_sum[: rows * cols] + fold).astype(BF16).reshape(rows, cols, chan)

    pl.when(has_up)(fg_up.start)
    fg_t[...] = fg[...].reshape(cells, chan).T
    pl.when(has_down)(fg_down.start)

    store_dec = pltpu.make_async_copy(dec_ref, dec_hbm, store_sem.at[0])
    store_ig = pltpu.make_async_copy(ig_ref, ig_hbm, store_sem.at[1])

    def store_tap(tap):
        g, t = tap // per_group, tap % per_group
        to = sg_hbm.at[tap] if tap < 9 else tg_hbm.at[tap - 9]
        source = turned.at[tap] if tap < 9 else full.at[g, t * chan : (t + 1) * chan]
        return pltpu.make_async_copy(source, to, store_sem.at[2 + tap])

    def make_decoded(start, count):
        def earlier(back):
            begin_at = start - back
            parts = []
            if begin_at < 0:
                parts.append(soh[2 + begin_at :])
            if begin_at + count > 0:
                parts.append(so[max(begin_at, 0) : begin_at + count])
            value = parts[0] if len(parts) == 1 else jnp.concatenate(parts, axis=0)
            return value.reshape(-1, chan)

        total = dot_nn(earlier(0), wt_ref[2])
        total += dot_nn(earlier(1), wt_ref[1])
        total += dot_nn(earlier(2), wt_ref[0])
        total += x_ref[start : start + count].astype(F32).reshape(-1, chan)
        dec_ref[start : start + count] = total.astype(BF16).reshape(count, rows, cols, chan)

    def decoded_later():
        make_decoded(2, frames - 2)

    def decoded_earlier():
        @pl.when(has_prev)
        def _():
            so_next.wait_recv()

        @pl.when(jnp.logical_not(has_prev))
        def _():
            soh[0] = so[0]
            soh[1] = so[0]

        make_decoded(0, 2)
        store_dec.start()

    def grad_taps_inner():
        taps(t_buf, 1, fg[...].astype(F32), rows, True)

    def grad_taps_outer():
        @pl.when(has_up)
        def _():
            fg_down.wait_recv()

        @pl.when(jnp.logical_not(has_up))
        def _():
            fgh[0] = jnp.zeros((frames, cols, chan), BF16)

        @pl.when(has_down)
        def _():
            fg_up.wait_recv()

        @pl.when(jnp.logical_not(has_down))
        def _():
            fgh[1] = jnp.zeros((frames, cols, chan), BF16)

        taps(t_buf, 0, fgh[0].astype(F32), 1, True)
        taps(t_buf, rows + 1, fgh[1].astype(F32), 1, True)

    def make_input_grad(start, count):
        total = None
        span = slice(start, start + count)
        for i in range(3):
            for j in range(3):
                left = t_buf[span, 2 - i : 2 - i + rows, :, j * chan : (j + 1) * chan]
                term = dot_nt(left.reshape(-1, chan), ws_ref[i, j * chan : (j + 1) * chan])
                total = term if total is None else total + term
        x = x_ref[span].astype(F32).reshape(-1, chan)
        s = sigmoid(x)
        grad = c_ref[span].astype(F32).reshape(-1, chan) + s * (1.0 + x * (1.0 - s)) * total
        ig_ref[span] = grad.astype(BF16).reshape(count, rows, cols, chan)

    def gather(g, level):
        copies = gather_copies(g, level)
        if level < 2:
            for copy in copies if level == 0 else copies[:1]:
                copy.wait_recv()
            start_all(gather_copies(g, level + 1))
            return
        gather_copies(g, 1)[1].wait_recv()
        copies[0].wait_recv()
        for t in range(per_group):
            tap = per_group * g + t
            if tap < 9:
                turned[tap] = full[g, t * chan : (t + 1) * chan].T
            store_tap(tap).start()

    def terms(g):
        for tap in range(per_group * g, per_group * g + per_group):
            temporal_term(tap) if tap >= 9 else spatial_term(tap)
        begin(g)

    events = []
    for n, g in enumerate(ORDER):
        if n > 0:
            events.append((n, functools.partial(terms, g)))
        for step in range(steps):
            after = (2, 5, 8)[step] if step < 3 else 8 + 4 * (step - 2)
            events.append((n + after + 0.1, functools.partial(advance, g, step)))
        for level in range(3):
            after = 8 + 4 * (steps - 3) + 3 * (level + 1)
            events.append((n + after + 0.2, functools.partial(gather, g, level)))
    units = [decoded_later, grad_taps_inner, decoded_earlier, grad_taps_outer]
    units += [functools.partial(make_input_grad, f, 1) for f in range(frames)] + [store_ig.start]
    for n, unit in enumerate(units):
        events.append((GROUPS + 0.5 + n, unit))
    for _, event in sorted(events, key=lambda e: e[0]):
        event()

    pl.when(has_prev)(c_prev.wait_send)
    pl.when(has_next)(so_next.wait_send)
    for up, down in ((x_up, x_down), (fg_up, fg_down)):
        pl.when(has_up)(up.wait_send)
        pl.when(has_down)(down.wait_send)
    for g in range(GROUPS):
        for step in range(steps):
            for copy in scatter_copies(g, step):
                copy.wait_send()
        for level in range(3):
            for copy in gather_copies(g, level):
                copy.wait_send()
    store_dec.wait()
    store_ig.wait()
    for tap in range(12):
        store_tap(tap).wait()


def write_out(*refs):
    ins, outs, held, sem = refs[:4], refs[4:8], refs[8:12], refs[12]
    parts = [(n, pl.ds(i, 3)) for n in (2, 3) for i in range(0, ins[n].shape[0], 3)]
    parts += [(n, pl.ds(0, ins[n].shape[0])) for n in (0, 1)]

    def copies(source, target, row):
        return [
            pltpu.make_async_copy(source[n].at[at], target[n].at[at], sem.at[row, k])
            for k, (n, at) in enumerate(parts)
        ]

    loads, stores = copies(ins, held, 0), copies(held, outs, 1)
    for load in loads:
        load.start()
    for load, store in zip(loads, stores):
        load.wait()
        store.start()
    for store in stores:
        store.wait()


def local(sizes, frames_in, cotangent, w_spatial, w_temporal):
    x, c = frames_in[0], cotangent[0]
    frames, rows, cols, chan = x.shape
    cell_count = frames * rows * cols * sizes["tm"] * sizes["height"] * sizes["dp"]
    group_rows = 12 * chan // GROUPS
    far = len(far_bits(sizes))
    buffer_rows = group_rows * 3 // 4 + (3 + far) * (group_rows // 16)
    exchanges = 5 + far + 6
    block = jax.ShapeDtypeStruct(x.shape, BF16)
    hbm = pl.BlockSpec(memory_space=pltpu.HBM)
    results = pl.pallas_call(
        functools.partial(kernel, sizes, 1.0 / math.sqrt(cell_count)),
        out_shape=(
            block,
            block,
            jax.ShapeDtypeStruct((9, chan, chan), BF16),
            jax.ShapeDtypeStruct((3, chan, chan), BF16),
        ),
        in_specs=[hbm] * 4,
        out_specs=(hbm,) * 4,
        scratch_shapes=[
            pltpu.VMEM(x.shape, BF16),
            pltpu.VMEM(x.shape, BF16),
            pltpu.VMEM(x.shape, BF16),
            pltpu.VMEM(x.shape, BF16),
            pltpu.VMEM((3, 3 * chan, chan), BF16),
            pltpu.VMEM(w_temporal.shape, BF16),
            pltpu.VMEM((2, frames, cols, chan), BF16),
            pltpu.VMEM((2, rows, cols, chan), BF16),
            pltpu.VMEM((2, rows, cols, chan), BF16),
            pltpu.VMEM((2, frames, cols, chan), BF16),
            pltpu.VMEM(x.shape, BF16),
            pltpu.VMEM(x.shape, BF16),
            pltpu.VMEM((frames, rows + 2, cols, 3 * chan), BF16),
            pltpu.VMEM((frames, rows + 2, cols, 3 * chan), BF16),
            pltpu.VMEM((GROUPS, group_rows, chan), F32),
            pltpu.VMEM((GROUPS, buffer_rows, chan), BF16),
            pltpu.VMEM((GROUPS, buffer_rows, chan), BF16),
            pltpu.VMEM((GROUPS, group_rows, chan), BF16),
            pltpu.VMEM((9, chan, chan), BF16),
            pltpu.VMEM((chan, frames * rows * cols), BF16),
            pltpu.VMEM((chan, frames * rows * cols), BF16),
            pltpu.SemaphoreType.DMA((4,)),
            pltpu.SemaphoreType.DMA((14,)),
            pltpu.SemaphoreType.DMA((6,)),
            pltpu.SemaphoreType.DMA((6,)),
            pltpu.SemaphoreType.DMA((GROUPS, exchanges)),
            pltpu.SemaphoreType.DMA((GROUPS, exchanges)),
        ],
        compiler_params=pltpu.CompilerParams(
            collective_id=0, has_side_effects=True, vmem_limit_bytes=VMEM_LIMIT
        ),
    )(x, c, w_spatial.reshape(3, 3 * chan, chan), w_temporal)
    decoded, input_grad, spatial, temporal = pl.pallas_call(
        write_out,
        out_shape=tuple(jax.ShapeDtypeStruct(r.shape, r.dtype) for r in results),
        in_specs=[hbm] * 4,
        out_specs=(hbm,) * 4,
        scratch_shapes=[pltpu.VMEM(r.shape, r.dtype) for r in results]
        + [pltpu.SemaphoreType.DMA((2, 6))],
        compiler_params=pltpu.CompilerParams(vmem_limit_bytes=VMEM_LIMIT),
    )(*results)
    return (
        decoded[None],
        input_grad[None],
        spatial.reshape(3, 3, chan, chan),
        temporal.reshape(3, chan, chan),
    )


def solution(mesh):
    sizes = dict(mesh.shape)
    spec = P("dp", "tm", "height", None, None)
    return jax.shard_map(
        functools.partial(local, sizes),
        mesh=mesh,
        in_specs=(spec, spec, P(), P()),
        out_specs=(spec, spec, P(), P()),
        check_vma=False,
    )
```

```python
import functools
import math

import jax
import jax.numpy as jnp
from jax import lax
from jax.experimental import pallas as pl
from jax.experimental.pallas import tpu as pltpu
from jax.sharding import PartitionSpec as P

F32 = jnp.float32
BF16 = jnp.bfloat16
GROUPS = 6
ORDER = (5, 4, 0, 1, 2, 3)
VMEM_LIMIT = 60 * 1024 * 1024


def split_bit(axis, distance):
    return lax.rem(lax.div(lax.axis_index(axis), distance), 2)


def across(*flips):
    place = {}
    for axis, distance in flips:
        index = place.get(axis, lax.axis_index(axis))
        place[axis] = index + distance - 2 * distance * split_bit(axis, distance)
    return place


NEAR = (("tm", 1), ("height", 1), ("tm", 2))


def far_bits(sizes):
    return [
        (axis, 1 << b)
        for axis in ("tm", "height")
        for b in range(sizes[axis].bit_length() - 1)
        if (axis, 1 << b) not in NEAR
    ]


def near_order(g):
    turn = g % len(NEAR)
    return NEAR[turn:] + NEAR[:turn]


def sigmoid(v):
    return 1.0 / (1.0 + jnp.exp(-v))


def shifted(v, cols):
    cells, ch = v.shape
    col = lax.broadcasted_iota(jnp.int32, (cells // cols, cols, ch), 1).reshape(cells, ch)
    before = jnp.where(col == 0, 0.0, pltpu.roll(v, 1, 0))
    after = jnp.where(col == cols - 1, 0.0, pltpu.roll(v, cells - 1, 0))
    return before, after


def dot_nn(a, b):
    return jnp.dot(a, b, preferred_element_type=F32)


def dot_nt(a, b):
    return lax.dot_general(a, b, (((1,), (1,)), ((), ())), preferred_element_type=F32)


def dot_tn(a, b):
    return lax.dot_general(a, b, (((0,), (0,)), ((), ())), preferred_element_type=F32)


def kernel(
    sizes, scale,
    x_hbm, c_hbm, ws_hbm, wt_hbm,
    dec_hbm, ig_hbm, sg_hbm, tg_hbm,
    dec_ref, ig_ref,    x_ref, c_ref, ws_ref, wt_ref, xh, ch, soh, fgh, so, fg, s_buf, t_buf, acc, sb, rb, full, turned, so_t, fg_t,
    load_sem, store_sem, halo_send, halo_recv, sum_send, sum_recv,
):
    frames, rows, cols, chan = x_ref.shape
    cells = frames * rows * cols
    tm, height = lax.axis_index("tm"), lax.axis_index("height")
    n_tm, n_h = sizes["tm"], sizes["height"]
    far = far_bits(sizes)
    per_group = 12 // GROUPS
    group_rows = per_group * chan
    half, quarter, own = group_rows // 2, group_rows // 4, group_rows // 16

    has_prev, has_next = tm > 0, tm < n_tm - 1
    has_up, has_down = height > 0, height < n_h - 1

    loads = [
        pltpu.make_async_copy(src, dst, load_sem.at[n])
        for n, (src, dst) in enumerate(
            ((x_hbm, x_ref), (ws_hbm, ws_ref), (c_hbm, c_ref), (wt_hbm, wt_ref))
        )
    ]
    for load in loads:
        load.start()

    barrier = pltpu.get_barrier_semaphore()

    def greet(device):
        pl.semaphore_signal(barrier, inc=1, device_id=device, device_id_type=pl.DeviceIdType.MESH)

    pairs = [(NEAR[0], NEAR[1]), (NEAR[1], NEAR[2]), (NEAR[2], NEAR[0])]
    partners = [(bit,) for bit in ((("dp", 1),) + NEAR + tuple(far))] + pairs
    for flips in partners:
        greet(across(*flips))
    pl.when(has_prev)(lambda: greet({"tm": tm - 1}))
    pl.when(has_next)(lambda: greet({"tm": tm + 1}))
    pl.when(has_up)(lambda: greet({"height": height - 1}))
    pl.when(has_down)(lambda: greet({"height": height + 1}))
    expected = len(partners) + sum(
        jnp.where(has, 1, 0) for has in (has_prev, has_next, has_up, has_down)
    )
    pl.semaphore_wait(barrier, expected)

    def remote(src, dst, sems, device):
        return pltpu.make_async_remote_copy(
            src_ref=src, dst_ref=dst, send_sem=sems[0], recv_sem=sems[1],
            device_id=device, device_id_type=pl.DeviceIdType.MESH,
        )

    def halo(at):
        return halo_send.at[at], halo_recv.at[at]

    x_up = remote(x_hbm.at[:, 0], xh.at[1], halo(0), {"height": height - 1})
    x_down = remote(x_hbm.at[:, rows - 1], xh.at[0], halo(1), {"height": height + 1})
    c_prev = remote(c_hbm.at[pl.ds(0, 2)], ch, halo(2), {"tm": tm - 1})
    so_next = remote(so.at[pl.ds(frames - 2, 2)], soh, halo(3), {"tm": tm + 1})
    fg_up = remote(fg.at[:, 0], fgh.at[1], halo(4), {"height": height - 1})
    fg_down = remote(fg.at[:, rows - 1], fgh.at[0], halo(5), {"height": height + 1})

    pl.when(has_prev)(c_prev.start)
    pl.when(has_up)(x_up.start)
    pl.when(has_down)(x_down.start)

    def taps(buf, part, value, count, flip):
        value = value.reshape(-1, chan)
        before, after = shifted(value, cols)
        if flip:
            before, after = after, before
        for j, v in enumerate((before, value, after)):
            v = v.astype(BF16).reshape(frames, count, cols, chan)
            buf[:, part : part + count, :, j * chan : (j + 1) * chan] = v

    def activation(v):
        v = v.astype(F32)
        return (v * sigmoid(v)).astype(BF16).astype(F32)

    loads[0].wait()
    taps(s_buf, 1, activation(x_ref[...]), rows, False)
    for load in loads[1:]:
        load.wait()

    @pl.when(has_up)
    def _():
        x_down.wait_recv()

    @pl.when(jnp.logical_not(has_up))
    def _():
        xh[0] = jnp.zeros((frames, cols, chan), BF16)

    @pl.when(has_down)
    def _():
        x_up.wait_recv()

    @pl.when(jnp.logical_not(has_down))
    def _():
        xh[1] = jnp.zeros((frames, cols, chan), BF16)

    taps(s_buf, 0, activation(xh[0]), 1, False)
    taps(s_buf, rows + 1, activation(xh[1]), 1, False)

    def s_rows(i):
        return s_buf[:, i : i + rows].reshape(cells, 3 * chan)

    out = dot_nn(s_rows(0), ws_ref[0])
    out += dot_nn(s_rows(1), ws_ref[1])
    out += dot_nn(s_rows(2), ws_ref[2])
    so[...] = out.astype(BF16).reshape(frames, rows, cols, chan)

    def put_term(tap, term):
        g, t = tap // per_group, tap % per_group
        acc[g, t * chan : (t + 1) * chan] = term * scale
        if tap in (9, 10):

            @pl.when(tm == 0)
            def _():
                so0 = so[0].reshape(-1, chan)
                extra = dot_tn(so0, c_ref[0].reshape(-1, chan))
                if tap == 9:
                    extra += dot_tn(so0, c_ref[1].reshape(-1, chan))
                acc[g, t * chan : (t + 1) * chan] += extra * scale

    def temporal_term(tap):
        put_term(tap, dot_nn(so_t[...], later(2 - (tap - 9))))

    def spatial_term(tap):
        i, j = tap // 3, tap % 3
        left = s_buf[:, i : i + rows, :, j * chan : (j + 1) * chan].reshape(cells, chan)
        put_term(tap, dot_nn(fg_t[...], left))

    def later(offset):
        if offset == 0:
            return c_ref[...].reshape(cells, chan)
        parts = [c_ref[offset:], ch[:offset]]
        return jnp.concatenate(parts, axis=0).reshape(cells, chan)

    so_t[...] = so[...].reshape(cells, chan).T
    temporal_term(11)

    @pl.when(has_next)
    def _():
        c_prev.wait_recv()

    @pl.when(jnp.logical_not(has_next))
    def _():
        ch[...] = jnp.zeros(ch.shape, BF16)

    def sum_copy(g, at, size, slot, flips):
        place = (g, pl.ds(at, size))
        sems = (sum_send.at[g, slot], sum_recv.at[g, slot])
        return remote(sb.at[place], rb.at[place], sems, across(*flips))

    def piece(start, size):
        return pl.ds(pl.multiple_of(start, size), size)

    def scatter_copies(g, step):
        first, second, third = near_order(g)
        if step == 0:
            return [sum_copy(g, 0, half, 0, [("dp", 1)])]
        if step == 1:
            return [sum_copy(g, half, quarter, 1, [first])]
        at = half + quarter
        if step == 2:
            return [
                sum_copy(g, at + n * own, own, 2 + n, flips)
                for n, flips in enumerate(([second], [third], [second, third]))
            ]
        return [sum_copy(g, at + step * own, own, 2 + step, [far[step - 3]])]

    steps = 3 + len(far)

    def kept(g):
        first, second, third = near_order(g)
        at_dp = split_bit("dp", 1) * half
        at_near = at_dp + split_bit(*first) * quarter
        return at_dp, at_near, at_near + (2 * split_bit(*second) + split_bit(*third)) * own

    def start_all(copies):
        for copy in copies:
            copy.start()

    def begin(g):
        sb[g, :half] = acc[g, piece((1 - split_bit("dp", 1)) * half, half)].astype(BF16)
        start_all(scatter_copies(g, 0))

    def advance(g, step):
        for copy in scatter_copies(g, step):
            copy.wait_recv()
        first, second, third = near_order(g)
        at_dp, at_near, at_own = kept(g)
        if step == 0:
            bit = split_bit(*first)
            away, stay = (1 - bit) * quarter, bit * quarter
            total = acc[g, piece(at_dp + away, quarter)] + rb[g, piece(away, quarter)].astype(F32)
            sb[g, half : half + quarter] = total.astype(BF16)
            start_all(scatter_copies(g, 1))
            acc[g, piece(at_dp + stay, quarter)] += rb[g, piece(stay, quarter)].astype(F32)
        elif step == 1:
            acc[g, piece(at_near, quarter)] += rb[g, half : half + quarter].astype(F32)
            b2, b3 = split_bit(*second), split_bit(*third)
            at = half + quarter
            for n, (p, q) in enumerate(((1 - b2, b3), (b2, 1 - b3), (1 - b2, 1 - b3))):
                away = acc[g, piece(at_near + (2 * p + q) * own, own)]
                sb[g, at + n * own : at + (n + 1) * own] = away.astype(BF16)
            start_all(scatter_copies(g, 2))
        else:
            at = half + quarter
            if step == 2:
                total = acc[g, piece(at_own, own)]
                for n in range(3):
                    total += rb[g, at + n * own : at + (n + 1) * own].astype(F32)
            else:
                here = slice(at + step * own, at + (step + 1) * own)
                total = sb[g, here].astype(F32) + rb[g, here].astype(F32)
            if step < steps - 1:
                sb[g, at + (step + 1) * own : at + (step + 2) * own] = total.astype(BF16)
                start_all(scatter_copies(g, step + 1))
            else:
                full[g, piece(at_own, own)] = total.astype(BF16)
                start_all(gather_copies(g, 0))

    def gather_copies(g, level):
        first, second, third = near_order(g)
        _, at_near, at_own = kept(g)

        def copy(place, slot, flips):
            block = full.at[g, place]
            slot += 2 + steps
            sems = (sum_send.at[g, slot], sum_recv.at[g, slot])
            return remote(block, block, sems, across(*flips))

        if level == 0:
            return [
                copy(piece(at_own, own), n, flips)
                for n, flips in enumerate(([second], [third], [second, third]))
            ]
        if level == 1:
            block = piece(at_near, quarter)
            return [copy(block, 3, [first]), copy(block, 4, [("dp", 1)])]
        other = split_bit("dp", 1) * half + (1 - split_bit(*first)) * quarter
        return [copy(piece(other, quarter), 5, [("dp", 1)])]

    temporal_term(10)
    begin(ORDER[0])

    fg_sum = dot_nt(later(0), wt_ref[2])
    fg_sum += dot_nt(later(1), wt_ref[1])
    fg_sum += dot_nt(later(2), wt_ref[0])
    fg[...] = fg_sum.astype(BF16).reshape(frames, rows, cols, chan)

    @pl.when(tm == 0)
    def _():
        c0 = c_ref[0].reshape(-1, chan)
        c1 = c_ref[1].reshape(-1, chan)
        fold = dot_nt(c0, wt_ref[0]) + dot_nt(c0, wt_ref[1]) + dot_nt(c1, wt_ref[0])
        fg[0] = (fg_sum[: rows * cols] + fold).astype(BF16).reshape(rows, cols, chan)

    fg_t[...] = fg[...].reshape(cells, chan).T

    store_dec = pltpu.make_async_copy(dec_ref, dec_hbm, store_sem.at[0])
    store_ig = pltpu.make_async_copy(ig_ref, ig_hbm, store_sem.at[1])

    def store_tap(tap):
        g, t = tap // per_group, tap % per_group
        to = sg_hbm.at[tap] if tap < 9 else tg_hbm.at[tap - 9]
        source = turned.at[tap] if tap < 9 else full.at[g, t * chan : (t + 1) * chan]
        return pltpu.make_async_copy(source, to, store_sem.at[2 + tap])

    def make_decoded(start, count):
        def earlier(back):
            begin_at = start - back
            parts = []
            if begin_at < 0:
                parts.append(soh[2 + begin_at :])
            if begin_at + count > 0:
                parts.append(so[max(begin_at, 0) : begin_at + count])
            value = parts[0] if len(parts) == 1 else jnp.concatenate(parts, axis=0)
            return value.reshape(-1, chan)

        total = dot_nn(earlier(0), wt_ref[2])
        total += dot_nn(earlier(1), wt_ref[1])
        total += dot_nn(earlier(2), wt_ref[0])
        total += x_ref[start : start + count].astype(F32).reshape(-1, chan)
        dec_ref[start : start + count] = total.astype(BF16).reshape(count, rows, cols, chan)

    def decoded_later():
        make_decoded(2, frames - 2)

    def decoded_earlier():
        @pl.when(has_prev)
        def _():
            so_next.wait_recv()

        @pl.when(jnp.logical_not(has_prev))
        def _():
            soh[0] = so[0]
            soh[1] = so[0]

        make_decoded(0, 2)
        store_dec.start()

    def grad_taps_inner():
        taps(t_buf, 1, fg[...].astype(F32), rows, True)

    def grad_taps_outer():
        @pl.when(has_up)
        def _():
            fg_down.wait_recv()

        @pl.when(jnp.logical_not(has_up))
        def _():
            fgh[0] = jnp.zeros((frames, cols, chan), BF16)

        @pl.when(has_down)
        def _():
            fg_up.wait_recv()

        @pl.when(jnp.logical_not(has_down))
        def _():
            fgh[1] = jnp.zeros((frames, cols, chan), BF16)

        taps(t_buf, 0, fgh[0].astype(F32), 1, True)
        taps(t_buf, rows + 1, fgh[1].astype(F32), 1, True)

    def make_input_grad(start, count):
        total = None
        span = slice(start, start + count)
        for i in range(3):
            for j in range(3):
                left = t_buf[span, 2 - i : 2 - i + rows, :, j * chan : (j + 1) * chan]
                term = dot_nt(left.reshape(-1, chan), ws_ref[i, j * chan : (j + 1) * chan])
                total = term if total is None else total + term
        x = x_ref[span].astype(F32).reshape(-1, chan)
        s = sigmoid(x)
        grad = c_ref[span].astype(F32).reshape(-1, chan) + s * (1.0 + x * (1.0 - s)) * total
        ig_ref[span] = grad.astype(BF16).reshape(count, rows, cols, chan)

    def gather(g, level):
        copies = gather_copies(g, level)
        if level < 2:
            for copy in copies if level == 0 else copies[:1]:
                copy.wait_recv()
            start_all(gather_copies(g, level + 1))
            return
        gather_copies(g, 1)[1].wait_recv()
        copies[0].wait_recv()
        for t in range(per_group):
            tap = per_group * g + t
            if tap < 9:
                turned[tap] = full[g, t * chan : (t + 1) * chan].T
            store_tap(tap).start()

    def terms(g):
        for tap in range(per_group * g, per_group * g + per_group):
            temporal_term(tap) if tap >= 9 else spatial_term(tap)
        begin(g)

    events = []
    for n, g in enumerate(ORDER):
        if n > 0:
            events.append((n, functools.partial(terms, g)))
        for step in range(steps):
            after = (2, 5, 8)[step] if step < 3 else 8 + 4 * (step - 2)
            events.append((n + after + 0.1, functools.partial(advance, g, step)))
        for level in range(3):
            after = 8 + 4 * (steps - 3) + 3 * (level + 1)
            events.append((n + after + 0.2, functools.partial(gather, g, level)))
    def send_frame_grad():
        pl.when(has_up)(fg_up.start)
        pl.when(has_down)(fg_down.start)

    def send_spatial_out():
        pl.when(has_next)(so_next.start)

    events += [
        (5.6, send_frame_grad), (6.5, decoded_later), (7.7, send_spatial_out),
        (8.5, grad_taps_inner), (11.5, grad_taps_outer), (17.5, decoded_earlier),
    ]
    events += [(12.5 + f, functools.partial(make_input_grad, f, 1)) for f in range(frames)]
    events.append((12.5 + frames, store_ig.start))
    for _, event in sorted(events, key=lambda e: e[0]):
        event()

    pl.when(has_prev)(c_prev.wait_send)
    pl.when(has_next)(so_next.wait_send)
    for up, down in ((x_up, x_down), (fg_up, fg_down)):
        pl.when(has_up)(up.wait_send)
        pl.when(has_down)(down.wait_send)
    for g in range(GROUPS):
        for step in range(steps):
            for copy in scatter_copies(g, step):
                copy.wait_send()
        for level in range(3):
            for copy in gather_copies(g, level):
                copy.wait_send()
    store_dec.wait()
    store_ig.wait()
    for tap in range(12):
        store_tap(tap).wait()


def write_out(*refs):
    ins, outs, held, sem = refs[:4], refs[4:8], refs[8:12], refs[12]
    parts = [(n, pl.ds(i, 3)) for n in (2, 3) for i in range(0, ins[n].shape[0], 3)]
    parts += [(n, pl.ds(0, ins[n].shape[0])) for n in (0, 1)]

    def copies(source, target, row):
        return [
            pltpu.make_async_copy(source[n].at[at], target[n].at[at], sem.at[row, k])
            for k, (n, at) in enumerate(parts)
        ]

    loads, stores = copies(ins, held, 0), copies(held, outs, 1)
    for load in loads:
        load.start()
    for load, store in zip(loads, stores):
        load.wait()
        store.start()
    for store in stores:
        store.wait()


def local(sizes, frames_in, cotangent, w_spatial, w_temporal):
    x, c = frames_in[0], cotangent[0]
    frames, rows, cols, chan = x.shape
    cell_count = frames * rows * cols * sizes["tm"] * sizes["height"] * sizes["dp"]
    group_rows = 12 * chan // GROUPS
    far = len(far_bits(sizes))
    buffer_rows = group_rows * 3 // 4 + (3 + far) * (group_rows // 16)
    exchanges = 5 + far + 6
    block = jax.ShapeDtypeStruct(x.shape, BF16)
    hbm = pl.BlockSpec(memory_space=pltpu.HBM)
    results = pl.pallas_call(
        functools.partial(kernel, sizes, 1.0 / math.sqrt(cell_count)),
        out_shape=(
            block,
            block,
            jax.ShapeDtypeStruct((9, chan, chan), BF16),
            jax.ShapeDtypeStruct((3, chan, chan), BF16),
        ),
        in_specs=[hbm] * 4,
        out_specs=(hbm,) * 4,
        scratch_shapes=[
            pltpu.VMEM(x.shape, BF16),
            pltpu.VMEM(x.shape, BF16),
            pltpu.VMEM(x.shape, BF16),
            pltpu.VMEM(x.shape, BF16),
            pltpu.VMEM((3, 3 * chan, chan), BF16),
            pltpu.VMEM(w_temporal.shape, BF16),
            pltpu.VMEM((2, frames, cols, chan), BF16),
            pltpu.VMEM((2, rows, cols, chan), BF16),
            pltpu.VMEM((2, rows, cols, chan), BF16),
            pltpu.VMEM((2, frames, cols, chan), BF16),
            pltpu.VMEM(x.shape, BF16),
            pltpu.VMEM(x.shape, BF16),
            pltpu.VMEM((frames, rows + 2, cols, 3 * chan), BF16),
            pltpu.VMEM((frames, rows + 2, cols, 3 * chan), BF16),
            pltpu.VMEM((GROUPS, group_rows, chan), F32),
            pltpu.VMEM((GROUPS, buffer_rows, chan), BF16),
            pltpu.VMEM((GROUPS, buffer_rows, chan), BF16),
            pltpu.VMEM((GROUPS, group_rows, chan), BF16),
            pltpu.VMEM((9, chan, chan), BF16),
            pltpu.VMEM((chan, frames * rows * cols), BF16),
            pltpu.VMEM((chan, frames * rows * cols), BF16),
            pltpu.SemaphoreType.DMA((4,)),
            pltpu.SemaphoreType.DMA((14,)),
            pltpu.SemaphoreType.DMA((6,)),
            pltpu.SemaphoreType.DMA((6,)),
            pltpu.SemaphoreType.DMA((GROUPS, exchanges)),
            pltpu.SemaphoreType.DMA((GROUPS, exchanges)),
        ],
        compiler_params=pltpu.CompilerParams(
            collective_id=0, has_side_effects=True, vmem_limit_bytes=VMEM_LIMIT
        ),
    )(x, c, w_spatial.reshape(3, 3 * chan, chan), w_temporal)
    decoded, input_grad, spatial, temporal = pl.pallas_call(
        write_out,
        out_shape=tuple(jax.ShapeDtypeStruct(r.shape, r.dtype) for r in results),
        in_specs=[hbm] * 4,
        out_specs=(hbm,) * 4,
        scratch_shapes=[pltpu.VMEM(r.shape, r.dtype) for r in results]
        + [pltpu.SemaphoreType.DMA((2, 6))],
        compiler_params=pltpu.CompilerParams(vmem_limit_bytes=VMEM_LIMIT),
    )(*results)
    return (
        decoded[None],
        input_grad[None],
        spatial.reshape(3, 3, chan, chan),
        temporal.reshape(3, chan, chan),
    )


def solution(mesh):
    sizes = dict(mesh.shape)
    spec = P("dp", "tm", "height", None, None)
    return jax.shard_map(
        functools.partial(local, sizes),
        mesh=mesh,
        in_specs=(spec, spec, P(), P()),
        out_specs=(spec, spec, P(), P()),
        check_vma=False,
    )
```
